32 devices in a mesh: fsdp: 2 (over x), ctx: 4 (over y, core), tp: 4 (over z).
Axes of the slice: x: 2, y: 2, z: 4, core: 2. Of those that a mesh axis runs over, the one named last changes fastest.
Arguments:
- tokens: bfloat16 [4, 2048, 1024], P('fsdp', ('ctx', 'tp')), may hold values from -6 to 6
- enc_states: bfloat16 [4, 256, 1024], P('fsdp', ('ctx', 'tp')), may hold values from -6 to 6
- enc_lengths: int32 [4], P('fsdp'), may hold values from 128 to 256, as said below
- cotangent: bfloat16 [4, 2048, 1024], P('fsdp', ('ctx', 'tp')), may hold values from -6 to 6
- gain_self: float32 [1024], replicated, may hold values from 0.25 to 1.75
- shift_self: float32 [1024], replicated, may hold values from -1.5 to 1.5
- w_query: bfloat16 [1024, 1024], P('fsdp', 'tp'), may hold values from -0.09375 to 0.09375
- w_key: bfloat16 [1024, 1024], P('fsdp', 'tp'), may hold values from -0.09375 to 0.09375
- w_value: bfloat16 [1024, 1024], P('fsdp', 'tp'), may hold values from -0.1875 to 0.1875
- w_out: bfloat16 [1024, 1024], P('tp', 'fsdp'), may hold values from -0.75 to 0.75
- gain_cross: float32 [1024], replicated, may hold values from 0.25 to 1.75
- shift_cross: float32 [1024], replicated, may hold values from -1.5 to 1.5
- cross_query: bfloat16 [1024, 1024], P('fsdp', 'tp'), may hold values from -0.09375 to 0.09375
- cross_key: bfloat16 [1024, 1024], P('fsdp', 'tp'), may hold values from -0.09375 to 0.09375
- cross_value: bfloat16 [1024, 1024], P('fsdp', 'tp'), may hold values from -0.1875 to 0.1875
- cross_out: bfloat16 [1024, 1024], P('tp', 'fsdp'), may hold values from -0.75 to 0.75
- gain_ffn: float32 [1024], replicated, may hold values from 0.25 to 1.75
- shift_ffn: float32 [1024], replicated, may hold values from -1.5 to 1.5
- w_inner: bfloat16 [1024, 4096], P('fsdp', 'tp'), may hold values from -0.1875 to 0.1875
- w_outer: bfloat16 [4096, 1024], P('tp', 'fsdp'), may hold values from -0.09375 to 0.09375
Outputs:
- out_tokens: bfloat16 [4, 2048, 1024], P('fsdp', ('ctx', 'tp'))
- grad_tokens: float32 [4, 2048, 1024], P('fsdp', ('ctx', 'tp'))
- grad_enc: float32 [4, 256, 1024], P('fsdp', ('ctx', 'tp'))
- grad_gain_self: float32 [1024], replicated
- grad_shift_self: float32 [1024], replicated
- grad_query: float32 [1024, 1024], P('fsdp', 'tp')
- grad_key: float32 [1024, 1024], P('fsdp', 'tp')
- grad_value: float32 [1024, 1024], P('fsdp', 'tp')
- grad_w_out: float32 [1024, 1024], P('tp', 'fsdp')
- grad_gain_cross: float32 [1024], replicated
- grad_shift_cross: float32 [1024], replicated
- grad_cross_query: float32 [1024, 1024], P('fsdp', 'tp')
- grad_cross_key: float32 [1024, 1024], P('fsdp', 'tp')
- grad_cross_value: float32 [1024, 1024], P('fsdp', 'tp')
- grad_cross_out: float32 [1024, 1024], P('tp', 'fsdp')
- grad_gain_ffn: float32 [1024], replicated
- grad_shift_ffn: float32 [1024], replicated
- grad_inner: float32 [1024, 4096], P('fsdp', 'tp')
- grad_outer: float32 [4096, 1024], P('tp', 'fsdp')
The draws below stay inside these ranges and needn't reach their ends.
Inputs may be any that keep to these rules, and one draw needn't show every extreme that they name: `enc_lengths`: some sequence has all 256 encoder states valid in every draw.
All inputs are finite; a program needn't handle non-finite values.
Results may differ from the reference program's by a relative error of at most 0.023.
Values may be sent and summed in bfloat16 or wider, within the bound.
No kernel may reach another device: no remote copies, remote signals or barrier semaphores. Data moves between devices by JAX's collectives and lax.ppermute only.
A program may use at most 256 MiB of HBM per device.

```python
import jax
import jax.numpy as jnp
from jax import lax

D = 1024
HEADS = 16
HEAD_DIM = 64
FF = 4096
ENC = 256
SEQS = 4
LEN = 2048


def draw_enc_lengths(key, part):
    first_key, second_key = jax.random.split(jax.random.fold_in(key, 7))
    drawn = jax.random.randint(first_key, (SEQS,), ENC // 2, ENC + 1)
    place = jax.random.randint(second_key, (), 0, SEQS)
    return jnp.where(jnp.arange(SEQS) == place, ENC, drawn).astype(jnp.int32)


def spiked(values, stream_key, source, target, parts, factor):
    def block_of(axis_at):
        return (jnp.arange(values.shape[axis_at]) // (values.shape[axis_at] // parts)).reshape((-1,) + (1,) * (values.ndim - 1 - axis_at))

    first = jax.random.permutation(stream_key, parts)[block_of(target)]
    second = (block_of(target) + parts // 2) % parts
    return jnp.where((block_of(source) == first) | (block_of(source) == second), factor * values, values)


def steps_of(stream_key, dims, pieces, least, top_value):
    loudness, own = 1.0, jax.random.fold_in(stream_key, 6)
    for dim, blocks in pieces:
        heights = jnp.exp(jax.random.uniform(jax.random.fold_in(own, dim), (blocks,), jnp.float32, least / len(pieces), top_value / len(pieces)))
        loudness = loudness * jnp.repeat(heights, dims[dim] // blocks).reshape([-1 if axis == dim else 1 for axis in range(len(dims))])
    return loudness


def noise(key, shape, scale, limit, cuts=(), held_as=jnp.bfloat16):
    entries = scale * jax.random.normal(key, shape, jnp.float32)
    if cuts:
        entries = entries * steps_of(key, shape, cuts, -0.22, 0.18)
    return jnp.clip(entries, -limit, limit).astype(held_as)


def heavy_noise(key, extent, width, bound, cuts, heavy, kind=jnp.bfloat16):
    entries = width * jax.random.normal(key, extent, jnp.float32)
    if cuts:
        entries = entries * steps_of(key, extent, cuts, -0.22, 0.18)
    return jnp.clip(spiked(entries, jax.random.fold_in(key, 3), *heavy), -bound, bound).astype(kind)


def setup_inputs(seed: int = 0) -> dict:
    splits = jax.random.split(jax.random.key(seed), 21)
    return {
        "tokens": heavy_noise(splits[0], (SEQS, LEN, D), 1.0, 6.0, ((0, 2), (1, 16)), (0, 2, 2, 2.0)),
        "enc_states": noise(splits[1], (SEQS, ENC, D), 1.0, 6.0, ((0, 2), (1, 16))),
        "enc_lengths": draw_enc_lengths(jax.random.fold_in(splits[20], 71), 0),
        "cotangent": heavy_noise(splits[3], (SEQS, LEN, D), 1.0, 6.0, ((0, 2), (1, 16)), (0, 2, 2, 2.0)),
        "gain_self": jnp.clip(1.0 + 0.15 * jax.random.normal(splits[4], (D,), jnp.float32), 0.25, 1.75),
        "shift_self": noise(splits[5], (D,), 0.3, 1.5, (), jnp.float32),
        "w_query": noise(splits[6], (D, D), (4 * D) ** -0.5, 0.09375, ((0, 2), (1, 4))),
        "w_key": noise(splits[7], (D, D), (4 * D) ** -0.5, 0.09375, ((0, 2), (1, 4))),
        "w_value": noise(splits[8], (D, D), D ** -0.5, 0.1875, ((0, 2), (1, 4))),
        "w_out": noise(splits[9], (D, D), (D // 16) ** -0.5, 0.75, ((0, 4), (1, 2))),
        "gain_cross": jnp.clip(1.0 + 0.15 * jax.random.normal(splits[10], (D,), jnp.float32), 0.25, 1.75),
        "shift_cross": noise(splits[11], (D,), 0.3, 1.5, (), jnp.float32),
        "cross_query": noise(splits[12], (D, D), (4 * D) ** -0.5, 0.09375, ((0, 2), (1, 4))),
        "cross_key": noise(splits[13], (D, D), (4 * D) ** -0.5, 0.09375, ((0, 2), (1, 4))),
        "cross_value": noise(splits[14], (D, D), D ** -0.5, 0.1875, ((0, 2), (1, 4))),
        "cross_out": noise(splits[15], (D, D), (D // 16) ** -0.5, 0.75, ((0, 4), (1, 2))),
        "gain_ffn": jnp.clip(1.0 + 0.15 * jax.random.normal(splits[16], (D,), jnp.float32), 0.25, 1.75),
        "shift_ffn": noise(splits[17], (D,), 0.3, 1.5, (), jnp.float32),
        "w_inner": noise(splits[18], (D, FF), D ** -0.5, 0.1875, ((0, 2), (1, 4))),
        "w_outer": noise(splits[19], (FF, D), FF ** -0.5, 0.09375, ((0, 4), (1, 2))),
    }


@jax.custom_vjp
def low(v):
    return lax.optimization_barrier(v.astype(jnp.bfloat16)).astype(jnp.float32)

@jax.custom_vjp
def low_back(v):
    return v

def low_keep(v):
    return (low(v), None)

def low_pass(kept, grad):
    return (grad,)

def back_keep(v):
    return (v, None)

def back_low(kept, grad):
    return (low(grad),)
low.defvjp(low_keep, low_pass)
low_back.defvjp(back_keep, back_low)

def rounded_both(value):
    return low_back(low(value))

def matmul(left, right):
    return jnp.dot(left, right, precision=lax.Precision.HIGHEST)

def gelu_tanh(value):
    return 0.5 * value * (1.0 + jnp.tanh(0.7978845608 * (value + 0.044715 * value * value * value)))

def layer_norm(hidden, gain, shift):
    centre = hidden - lax.optimization_barrier(jnp.mean(hidden, axis=-1, keepdims=True))
    spread = lax.optimization_barrier(jnp.mean(centre * centre, axis=-1, keepdims=True))
    return centre * lax.rsqrt(spread + 1e-05) * gain + shift

def attend(queries, keys_in, values_in, allowed):
    q_heads = queries.reshape(queries.shape[0], HEADS, HEAD_DIM)
    k_heads = keys_in.reshape(keys_in.shape[0], HEADS, HEAD_DIM)
    v_heads = values_in.reshape(values_in.shape[0], HEADS, HEAD_DIM)
    scores = jnp.einsum('qhd,khd->hqk', q_heads, k_heads, precision=lax.Precision.HIGHEST) * HEAD_DIM ** (-0.5)
    scores = low_back(scores)
    scores = jnp.where(allowed[None], scores, -1000000000.0)
    row_top = lax.optimization_barrier(jnp.max(scores, axis=-1, keepdims=True))
    exponent = jnp.exp(scores - row_top)
    probs = exponent / lax.optimization_barrier(jnp.sum(exponent, axis=-1, keepdims=True))
    mixed = jnp.einsum('hqk,khd->qhd', low(probs), v_heads, precision=lax.Precision.HIGHEST)
    return rounded_both(mixed.reshape(queries.shape[0], HEADS * HEAD_DIM))

def layer_one(params, hidden0, encoder, length):
    gain_self, shift_self, w_query, w_key, w_value, w_out, gain_cross, shift_cross, cross_query, cross_key, cross_value, cross_out, gain_ffn, shift_ffn, w_inner, w_outer = params
    position = jnp.arange(LEN)
    causal = position[:, None] >= position[None, :]
    reach = jnp.broadcast_to((jnp.arange(ENC) < length)[None, :], (LEN, ENC))
    normed1 = low(layer_norm(hidden0, gain_self, shift_self))
    q_self = rounded_both(matmul(normed1, w_query))
    k_self = rounded_both(matmul(normed1, w_key))
    v_self = rounded_both(matmul(normed1, w_value))
    hidden1 = hidden0 + low_back(matmul(attend(q_self, k_self, v_self, causal), w_out))
    normed2 = low(layer_norm(hidden1, gain_cross, shift_cross))
    q_cross = rounded_both(matmul(normed2, cross_query))
    k_cross = rounded_both(matmul(encoder, cross_key))
    v_cross = rounded_both(matmul(encoder, cross_value))
    hidden2 = hidden1 + low_back(matmul(attend(q_cross, k_cross, v_cross, reach), cross_out))
    normed3 = low(layer_norm(hidden2, gain_ffn, shift_ffn))
    inner = low_back(matmul(normed3, w_inner))
    active = low(gelu_tanh(inner))
    return hidden2 + low_back(matmul(active, w_outer))

def reference(tokens, enc_states, enc_lengths, cotangent, gain_self, shift_self, w_query, w_key, w_value, w_out, gain_cross, shift_cross, cross_query, cross_key, cross_value, cross_out, gain_ffn, shift_ffn, w_inner, w_outer):
    params = tuple((p.astype(jnp.float32) for p in (gain_self, shift_self, w_query, w_key, w_value, w_out, gain_cross, shift_cross, cross_query, cross_key, cross_value, cross_out, gain_ffn, shift_ffn, w_inner, w_outer)))

    def forward(tok_in, enc_in, *weights):
        step_fn = jax.checkpoint(lambda item: layer_one(weights, item[0], item[1], item[2]))
        return lax.map(step_fn, (tok_in, enc_in, enc_lengths))
    result, pull = jax.vjp(forward, tokens.astype(jnp.float32), enc_states.astype(jnp.float32), *params)
    grads = pull(cotangent.astype(jnp.float32))
    return (result.astype(jnp.bfloat16), grads[0], grads[1], grads[2], grads[3], grads[4], grads[5], grads[6], grads[7], grads[8], grads[9], grads[10], grads[11], grads[12], grads[13], grads[14], grads[15], grads[16], grads[17])
```

```python
import functools

import jax
import jax.numpy as jnp
from jax import lax
from jax.experimental import pallas as pl
from jax.experimental.pallas import tpu as pltpu
from jax.sharding import PartitionSpec as P

HEAD_DIM = 64
SCALE = HEAD_DIM ** (-0.5)
BLOCK = 512
MASKED = -1e30
F32 = jnp.float32
BF16 = jnp.bfloat16
ROWS_ROWS = (((1,), (1,)), ((), ()))
ROWS_COLS = (((1,), (0,)), ((), ()))
COLS_COLS = (((0,), (0,)), ((), ()))


def dot(left, right, dims, precision=None):
    return lax.dot_general(left, right, dims, preferred_element_type=F32, precision=precision)


def self_kernel(block, order, qkv, out, lse, q_s, k_s, v_s):
    parts, rows, width = qkv.shape[0], qkv.shape[1], q_s.shape[1]
    for p in range(parts):
        r, at = order[p], slice(p * rows, (p + 1) * rows)
        q_s[at, :] = qkv[r, :, 0:width]
        k_s[at, :] = qkv[r, :, width : 2 * width]
        v_s[at, :] = qkv[r, :, 2 * width : 3 * width]
    lane = lax.broadcasted_iota(jnp.int32, (1, width), 1)
    row = lax.broadcasted_iota(jnp.int32, (block, block), 0)
    col = lax.broadcasted_iota(jnp.int32, (block, block), 1)
    for i in range(parts * rows // block):
        first, at = i * block, slice(i * block, (i + 1) * block)
        q = q_s[at, :]
        mixed = []
        for h in range(2):
            qh = jnp.where((lane < width // 2) == (h == 0), q, jnp.zeros_like(q))
            near = jnp.where(row >= col, dot(qh, k_s[at, :], ROWS_ROWS) * SCALE, MASKED)
            top = jnp.max(near, axis=1, keepdims=True)
            if first:
                far = dot(qh, k_s[0:first, :], ROWS_ROWS) * SCALE
                top = jnp.maximum(top, jnp.max(far, axis=1, keepdims=True))
                far = jnp.exp(far - top)
            near = jnp.exp(near - top)
            total = jnp.sum(near, axis=1, keepdims=True)
            acc = dot(near.astype(BF16), v_s[at, :], ROWS_COLS)
            if first:
                total = total + jnp.sum(far, axis=1, keepdims=True)
                acc = acc + dot(far.astype(BF16), v_s[0:first, :], ROWS_COLS)
            mixed.append(acc / total)
            flat = jnp.broadcast_to(top + jnp.log(total), (block, 128)).T
            lse[h : h + 1, at] = flat[0:1, :]
        both = jnp.where(lane < width // 2, mixed[0], mixed[1]).astype(BF16)
        for t in range(block // rows):
            out[order[i * (block // rows) + t]] = both[t * rows : (t + 1) * rows, :]


def self_attend(qkv, order):
    parts, rows, width = qkv.shape
    width //= 3
    length = parts * rows
    vmem = pl.BlockSpec(memory_space=pltpu.VMEM)
    return pl.pallas_call(
        functools.partial(self_kernel, BLOCK),
        out_shape=(
            jax.ShapeDtypeStruct((parts, rows, width), BF16),
            jax.ShapeDtypeStruct((2, length), F32),
        ),
        in_specs=[pl.BlockSpec(memory_space=pltpu.SMEM), vmem],
        out_specs=(vmem, vmem),
        scratch_shapes=[pltpu.VMEM((length, width), BF16)] * 3,
        compiler_params=pltpu.CompilerParams(vmem_limit_bytes=48 << 20),
        cost_estimate=pl.CostEstimate(
            flops=4 * length * length * width,
            bytes_accessed=8 * length * width,
            transcendentals=length * length,
        ),
        name="self_attend",
    )(order, qkv)


def self_back_kernel(block, order, qkv, out, lse, grad, grad_qkv, q_s, k_s, v_s, g_s, sum_s, dq_s):
    parts, rows, width = qkv.shape[0], qkv.shape[1], q_s.shape[1]
    length = parts * rows
    lane = lax.broadcasted_iota(jnp.int32, (1, width), 1)
    lane8 = lax.broadcasted_iota(jnp.int32, (8, width), 1)
    row8 = lax.broadcasted_iota(jnp.int32, (8, width), 0)
    pick = jnp.where(lane8 // (width // 2) == row8, 1.0, 0.0).astype(F32)
    for p in range(parts):
        r, at = order[p], slice(p * rows, (p + 1) * rows)
        q_s[at, :] = qkv[r, :, 0:width]
        k_s[at, :] = qkv[r, :, width : 2 * width]
        v_s[at, :] = qkv[r, :, 2 * width : 3 * width]
        g_s[at, :] = grad[r]
        sum_s[:, at] = dot(
            pick, grad[r].astype(F32) * out[r].astype(F32), ROWS_ROWS, lax.Precision.HIGHEST
        )
    row = lax.broadcasted_iota(jnp.int32, (block, block), 0)
    col = lax.broadcasted_iota(jnp.int32, (block, block), 1)
    dq_s[...] = jnp.zeros_like(dq_s)
    for j in range(length // block):
        kj, vj = k_s[j * block : (j + 1) * block, :], v_s[j * block : (j + 1) * block, :]
        dks, dvs = [], []
        for h in range(2):
            mine = (lane < width // 2) == (h == 0)
            kh = jnp.where(mine, kj, jnp.zeros_like(kj))
            vh = jnp.where(mine, vj, jnp.zeros_like(vj))
            dk = dv = None
            for i in range(j, length // block):
                at = slice(i * block, (i + 1) * block)
                q, g = q_s[at, :], g_s[at, :]
                scores = dot(kh, q, ROWS_ROWS) * SCALE - lse[h : h + 1, at]
                if i == j:
                    scores = jnp.where(col >= row, scores, MASKED)
                probs = jnp.exp(scores)
                ds = probs * (dot(vh, g, ROWS_ROWS) - sum_s[h : h + 1, at])
                ds = ds.astype(BF16)
                more_v, more_k = (
                    dot(probs.astype(BF16), g, ROWS_COLS),
                    dot(ds, q, ROWS_COLS),
                )
                dk, dv = (more_k, more_v) if dk is None else (dk + more_k, dv + more_v)
                dq_s[at, :] += dot(ds, kh, COLS_COLS)
            dks.append(dk)
            dvs.append(dv)
        dk = (jnp.where(lane < width // 2, dks[0], dks[1]) * SCALE).astype(BF16)
        dv = jnp.where(lane < width // 2, dvs[0], dvs[1]).astype(BF16)
        for t in range(block // rows):
            r, at = order[j * (block // rows) + t], slice(t * rows, (t + 1) * rows)
            grad_qkv[r, :, width : 2 * width] = dk[at]
            grad_qkv[r, :, 2 * width : 3 * width] = dv[at]
    for p in range(parts):
        grad_qkv[order[p], :, 0:width] = (dq_s[p * rows : (p + 1) * rows, :] * SCALE).astype(BF16)


def self_attend_back(qkv, out, lse, grad, order):
    parts, rows, width = qkv.shape
    width //= 3
    length = parts * rows
    vmem = pl.BlockSpec(memory_space=pltpu.VMEM)
    return pl.pallas_call(
        functools.partial(self_back_kernel, BLOCK),
        out_shape=jax.ShapeDtypeStruct(qkv.shape, BF16),
        in_specs=[pl.BlockSpec(memory_space=pltpu.SMEM), vmem, vmem, vmem, vmem],
        out_specs=vmem,
        scratch_shapes=[pltpu.VMEM((length, width), BF16)] * 4
        + [pltpu.VMEM((8, length), F32), pltpu.VMEM((length, width), F32)],
        compiler_params=pltpu.CompilerParams(vmem_limit_bytes=48 << 20),
        cost_estimate=pl.CostEstimate(
            flops=10 * length * length * width,
            bytes_accessed=16 * length * width,
            transcendentals=length * length,
        ),
        name="self_attend_back",
    )(order, qkv, out, lse, grad)


def cross_kernel(lengths, q_ref, k_ref, v_ref, out, lse):
    seqs, rows, width = q_ref.shape
    keys = k_ref.shape[1]
    lane = lax.broadcasted_iota(jnp.int32, (1, 128), 1)
    col = lax.broadcasted_iota(jnp.int32, (rows, keys), 1)
    for s in range(seqs):
        valid = col < lengths[s]
        for pair in range(width // 128):
            at = slice(pair * 128, (pair + 1) * 128)
            q, k, v = q_ref[s, :, at], k_ref[s, :, at], v_ref[s, :, at]
            mixed = []
            for h in range(2):
                qh = jnp.where((lane < 64) == (h == 0), q, jnp.zeros_like(q))
                scores = jnp.where(valid, dot(qh, k, ROWS_ROWS) * SCALE, MASKED)
                top = jnp.max(scores, axis=1, keepdims=True)
                probs = jnp.exp(scores - top)
                total = jnp.sum(probs, axis=1, keepdims=True)
                mixed.append(dot(probs.astype(BF16), v, ROWS_COLS) / total)
                flat = jnp.broadcast_to(top + jnp.log(total), (rows, 128)).T
                place = s * (width // 64) + pair * 2 + h
                lse[place : place + 1, :] = flat[0:1, :]
            out[s, :, at] = jnp.where(lane < 64, mixed[0], mixed[1]).astype(BF16)


def cross_attend(queries, keys_in, values_in, lengths):
    seqs, rows, width = queries.shape
    keys = keys_in.shape[1]
    vmem = pl.BlockSpec(memory_space=pltpu.VMEM)
    return pl.pallas_call(
        cross_kernel,
        out_shape=(
            jax.ShapeDtypeStruct(queries.shape, BF16),
            jax.ShapeDtypeStruct((seqs * width // 64, rows), F32),
        ),
        in_specs=[pl.BlockSpec(memory_space=pltpu.SMEM), vmem, vmem, vmem],
        out_specs=(vmem, vmem),
        compiler_params=pltpu.CompilerParams(vmem_limit_bytes=48 << 20),
        cost_estimate=pl.CostEstimate(
            flops=8 * seqs * rows * keys * width,
            bytes_accessed=4 * seqs * (rows + keys) * width,
            transcendentals=seqs * rows * keys * width // 64,
        ),
        name="cross_attend",
    )(lengths, queries, keys_in, values_in)


def cross_back_kernel(lengths, q_ref, k_ref, v_ref, lse, g_ref, dq_ref, dk_ref, dv_ref):
    seqs, rows, width = q_ref.shape
    keys = k_ref.shape[1]
    lane = lax.broadcasted_iota(jnp.int32, (1, 128), 1)
    row = lax.broadcasted_iota(jnp.int32, (keys, rows), 0)
    for s in range(seqs):
        valid = row < lengths[s]
        for pair in range(width // 128):
            at = slice(pair * 128, (pair + 1) * 128)
            q, k, v, g = q_ref[s, :, at], k_ref[s, :, at], v_ref[s, :, at], g_ref[s, :, at]
            dks, dvs, dq = [], [], None
            for h in range(2):
                mine = (lane < 64) == (h == 0)
                kh = jnp.where(mine, k, jnp.zeros_like(k))
                vh = jnp.where(mine, v, jnp.zeros_like(v))
                place = s * (width // 64) + pair * 2 + h
                scores = dot(kh, q, ROWS_ROWS) * SCALE - lse[place : place + 1, :]
                probs = jnp.exp(jnp.where(valid, scores, MASKED))
                dp = dot(vh, g, ROWS_ROWS)
                ds = (probs * (dp - jnp.sum(probs * dp, axis=0, keepdims=True))).astype(BF16)
                dvs.append(dot(probs.astype(BF16), g, ROWS_COLS))
                dks.append(dot(ds, q, ROWS_COLS))
                more = dot(ds, kh, COLS_COLS)
                dq = more if dq is None else dq + more
            dq_ref[s, :, at] = (dq * SCALE).astype(BF16)
            dk_ref[s, :, at] = (jnp.where(lane < 64, dks[0], dks[1]) * SCALE).astype(BF16)
            dv_ref[s, :, at] = jnp.where(lane < 64, dvs[0], dvs[1]).astype(BF16)


def cross_attend_back(queries, keys_in, values_in, lse, grad, lengths):
    seqs, rows, width = queries.shape
    keys = keys_in.shape[1]
    vmem = pl.BlockSpec(memory_space=pltpu.VMEM)
    return pl.pallas_call(
        cross_back_kernel,
        out_shape=(
            jax.ShapeDtypeStruct(queries.shape, BF16),
            jax.ShapeDtypeStruct(keys_in.shape, BF16),
            jax.ShapeDtypeStruct(keys_in.shape, BF16),
        ),
        in_specs=[pl.BlockSpec(memory_space=pltpu.SMEM)] + [vmem] * 5,
        out_specs=(vmem, vmem, vmem),
        compiler_params=pltpu.CompilerParams(vmem_limit_bytes=48 << 20),
        cost_estimate=pl.CostEstimate(
            flops=20 * seqs * rows * keys * width,
            bytes_accessed=8 * seqs * (rows + keys) * width,
            transcendentals=seqs * rows * keys * width // 64,
        ),
        name="cross_attend_back",
    )(lengths, queries, keys_in, values_in, lse, grad)


def swap_core(value):
    size = lax.axis_size("ctx")
    return lax.ppermute(value, "ctx", [(i, i ^ 1) for i in range(size)])


def swap_y(value):
    size = lax.axis_size("ctx")
    return lax.ppermute(value, "ctx", [(i, i ^ 2) for i in range(size)])


def from_tp(value, step):
    size = lax.axis_size("tp")
    return lax.ppermute(value, "tp", [((i + step) % size, i) for i in range(size)])


def gather_tp(value):
    return jnp.stack([value] + [from_tp(value, e) for e in range(1, lax.axis_size("tp"))])


def in_order(pieces, place):
    size = pieces.shape[0]
    return lax.dynamic_slice_in_dim(
        jnp.concatenate([pieces, pieces]), (size - place) % size, size, 0
    )


def gather_model(value):
    if lax.axis_size("fsdp") != 2:
        return lax.all_gather(value, "fsdp", axis=value.ndim - 1, tiled=True)
    other = lax.ppermute(value, "fsdp", [(0, 1), (1, 0)])
    return jnp.where(
        lax.axis_index("fsdp") == 0,
        jnp.concatenate([value, other], axis=-1),
        jnp.concatenate([other, value], axis=-1),
    )


def sum_model(value):
    if lax.axis_size("fsdp") != 2:
        return lax.psum_scatter(
            value.astype(BF16), "fsdp", scatter_dimension=value.ndim - 1, tiled=True
        ).astype(F32)
    width, mine = value.shape[-1] // 2, lax.axis_index("fsdp")
    keep = lax.dynamic_slice_in_dim(value, mine * width, width, value.ndim - 1)
    send = lax.dynamic_slice_in_dim(value, (1 - mine) * width, width, value.ndim - 1)
    return keep.astype(F32) + lax.ppermute(
        send.astype(BF16), "fsdp", [(0, 1), (1, 0)]
    ).astype(F32)


def sum_tp(pieces):
    size = pieces.shape[0]
    total = pieces[0].astype(F32)
    for e in range(1, size):
        total = total + from_tp(pieces[size - e].astype(BF16), e).astype(F32)
    return total


def pick(value, index, axis):
    return lax.dynamic_index_in_dim(value, index, axis, keepdims=False)


def layer_norm(hidden, gain, shift):
    centre = hidden - jnp.mean(hidden, axis=-1, keepdims=True)
    spread = jnp.mean(centre * centre, axis=-1, keepdims=True)
    return (centre * lax.rsqrt(spread + 1e-05) * gain + shift).astype(BF16)


def layer_norm_back(hidden, gain, grad):
    centre = hidden - jnp.mean(hidden, axis=-1, keepdims=True)
    rate = lax.rsqrt(jnp.mean(centre * centre, axis=-1, keepdims=True) + 1e-05)
    unit, scaled = centre * rate, grad * gain
    back = rate * (
        scaled
        - jnp.mean(scaled, axis=-1, keepdims=True)
        - unit * jnp.mean(scaled * unit, axis=-1, keepdims=True)
    )
    return back, jnp.sum(grad * unit, axis=(0, 1)), jnp.sum(grad, axis=(0, 1))


def gelu_tanh(value):
    return 0.5 * value * (1.0 + jnp.tanh(0.7978845608 * (value + 0.044715 * value * value * value)))


def onto(rows_in, weight):
    return lax.dot_general(
        rows_in, weight, (((rows_in.ndim - 1,), (1,)), ((), ())), preferred_element_type=F32
    )


def back_onto(rows_in, weight):
    return lax.dot_general(
        rows_in, weight, (((rows_in.ndim - 1,), (0,)), ((), ())), preferred_element_type=F32
    )


def weight_grad(grad_rows, rows_in):
    dims = tuple(range(rows_in.ndim - 1))
    return lax.dot_general(
        grad_rows, rows_in, ((dims, dims), ((), ())), preferred_element_type=F32
    )


def chip_rows(value):
    return jnp.stack([value, swap_core(value)], axis=1).reshape(
        value.shape[0], 2 * value.shape[1], value.shape[2]
    )


def sum_chip(value):
    seqs, rows, width = value.shape
    value = value.reshape(seqs, 2, rows // 2, width)
    return value[:, 0] + swap_core(value[:, 1].astype(BF16)).astype(F32)


def ctx_rows(value):
    near = jnp.stack([value, swap_core(value)])
    far = swap_y(value)
    far = jnp.stack([far, swap_core(far)])
    return jnp.concatenate([near, far]).reshape(-1, value.shape[-1])


def sum_ctx(value, shape):
    value = value.reshape((4,) + shape)
    got = swap_core(value[1::2].astype(BF16)).astype(F32)
    far = value[2] + got[1]
    return value[0] + got[0] + swap_y(far.astype(BF16)).astype(F32)


def shards(
    tokens,
    enc_states,
    enc_lengths,
    cotangent,
    gain_self,
    shift_self,
    w_query,
    w_key,
    w_value,
    w_out,
    gain_cross,
    shift_cross,
    cross_query,
    cross_key,
    cross_value,
    cross_out,
    gain_ffn,
    shift_ffn,
    w_inner,
    w_outer,
):
    seqs, rows, model = tokens.shape
    tp, ctx = lax.axis_size("tp"), lax.axis_size("ctx")
    z, c = lax.axis_index("tp"), lax.axis_index("ctx")
    y, k = c // 2, c % 2
    span = tp // 2
    half, low = z // span, z % span
    local = w_query.shape[0]
    hid = w_inner.shape[1] // ctx

    def core_half(weight):
        return pick(weight.reshape(2, 2, HEAD_DIM, local), k, 1).reshape(2 * HEAD_DIM, local)

    def own_head(weight):
        return lax.dynamic_slice_in_dim(weight, c * HEAD_DIM, HEAD_DIM, 0)

    hidden0 = tokens.astype(F32)
    n1 = layer_norm(hidden0, gain_self, shift_self)
    mine = pick(n1, half, 0)
    near = [mine] + [
        from_tp(pick(n1, ((z - e) % tp) // span, 0), e) for e in range(1, tp)
    ]
    far = [swap_y(piece) for piece in near]
    near, far = jnp.stack(near), jnp.stack(far)
    n1_all = [near, far, swap_core(near), swap_core(far)]

    own_qkv = jnp.stack([own_head(w.T) for w in (w_query, w_key, w_value)])
    other_qkv = from_tp(own_qkv, span)
    h_qkv = jnp.where(
        z < span, jnp.stack([own_qkv, other_qkv], 1), jnp.stack([other_qkv, own_qkv], 1)
    )
    h_qkv = gather_model(h_qkv.reshape(-1, local))

    h_out = in_order(gather_tp(core_half(w_out)), z)
    h_out = (
        h_out.reshape(2, span, 2, HEAD_DIM, local).transpose(1, 2, 0, 3, 4).reshape(-1, local)
    )
    h_out = gather_model(h_out)

    h_ckv = gather_model(jnp.concatenate([core_half(cross_key.T), core_half(cross_value.T)]))
    h_cq, h_cout = gather_model(
        gather_tp(jnp.stack([core_half(cross_query.T), core_half(cross_out)]))
        .transpose(1, 0, 2, 3)
        .reshape(2, -1, local)
    )
    quarter = jnp.stack(
        [
            lax.dynamic_slice_in_dim(w_inner, c * hid, hid, 1).T,
            lax.dynamic_slice_in_dim(w_outer, c * hid, hid, 0),
        ]
    )
    h_inner, h_outer = gather_model(
        gather_tp(quarter).transpose(1, 0, 2, 3).reshape(2, -1, local)
    )

    place = jnp.arange(ctx * tp)
    p_c, p_z = place // tp, place % tp
    order = (((p_c % 2) ^ k) * 2 + ((p_c // 2) ^ y)) * tp + (p_z - z) % tp
    order = order.astype(jnp.int32)
    qkv = jnp.concatenate([onto(part, h_qkv).astype(BF16) for part in n1_all])
    o_self, lse_self = self_attend(qkv, order)

    o_parts = o_self.reshape(2, 2, tp, rows, 2 * HEAD_DIM)
    came = jnp.stack(
        [o_parts[:, :, 0]] + [from_tp(o_parts[:, :, tp - e], e) for e in range(1, tp)]
    )
    here, there = came[:, :, 0], swap_y(came[:, :, 1])
    came = jnp.where(y == 0, jnp.stack([here, there], 1), jnp.stack([there, here], 1))
    came = in_order(came, z)
    o_chip = (
        came.reshape(seqs, span, 2, 2, rows, 2 * HEAD_DIM)
        .transpose(0, 3, 4, 1, 2, 5)
        .reshape(seqs, 2 * rows, -1)
    )
    hidden1 = hidden0 + sum_chip(back_onto(o_chip, h_out))

    enc_all = lax.all_gather(enc_states, ("ctx", "tp"), axis=1, tiled=True)
    kv = gather_tp(onto(enc_all, h_ckv).astype(BF16))
    kv = kv.reshape(tp, seqs, -1, 2, 2 * HEAD_DIM).transpose(3, 1, 2, 0, 4)
    k_cross, v_cross = kv.reshape(2, seqs, -1, tp * 2 * HEAD_DIM)
    n2 = chip_rows(layer_norm(hidden1, gain_cross, shift_cross))
    q_cross = onto(n2, h_cq).astype(BF16)
    o_cross, lse_cross = cross_attend(q_cross, k_cross, v_cross, enc_lengths)
    hidden2 = hidden1 + sum_chip(back_onto(o_cross, h_cout))

    grad3 = cotangent.astype(F32)
    dy_ffn = ctx_rows(cotangent)
    n3 = ctx_rows(layer_norm(hidden2, gain_ffn, shift_ffn))
    inner = onto(n3, h_inner)
    active, pull_gelu = jax.vjp(gelu_tanh, inner)
    active = active.astype(BF16)
    d_inner = pull_gelu(onto(dy_ffn, h_outer))[0].astype(BF16)
    d_n3 = sum_ctx(back_onto(d_inner, h_inner), tokens.shape)
    out_tokens = (hidden2 + sum_ctx(back_onto(active, h_outer), tokens.shape)).astype(BF16)

    g_ffn = jnp.stack([weight_grad(d_inner, n3), weight_grad(active, dy_ffn)])
    g_ffn = sum_model(g_ffn.reshape(2, tp, hid, model))
    g_ffn = sum_tp(g_ffn.transpose(1, 0, 2, 3)).astype(BF16)
    g_ffn = lax.all_gather(g_ffn, "ctx", axis=1, tiled=True)
    grad_inner, grad_outer = g_ffn[0].T.astype(F32), g_ffn[1].astype(F32)

    back_ffn, grad_gain_ffn, grad_shift_ffn = layer_norm_back(hidden2, gain_ffn, d_n3)
    grad2 = grad3 + back_ffn

    dy_cross = chip_rows(grad2.astype(BF16))
    do_cross = onto(dy_cross, h_cout).astype(BF16)
    dq_cross, dk_cross, dv_cross = cross_attend_back(
        q_cross, k_cross, v_cross, lse_cross, do_cross, enc_lengths
    )
    d_n2 = sum_chip(back_onto(dq_cross, h_cq))
    back_cross, grad_gain_cross, grad_shift_cross = layer_norm_back(hidden1, gain_cross, d_n2)
    grad1 = grad2 + back_cross

    d_kv = jnp.concatenate(
        [v.reshape(seqs, -1, tp, 2, HEAD_DIM) for v in (dk_cross, dv_cross)], axis=-1
    )
    d_kv = pick(d_kv, y, 3).astype(F32) + swap_y(pick(d_kv, 1 - y, 3)).astype(F32)
    d_kv = sum_tp(d_kv.transpose(2, 0, 1, 3)).astype(BF16)
    own_ckv = pick(h_ckv.reshape(2, 2, HEAD_DIM, model), y, 1).reshape(-1, model)
    grad_enc = lax.psum_scatter(
        back_onto(d_kv, own_ckv).astype(BF16), ("ctx", "tp"), scatter_dimension=1, tiled=True
    ).astype(F32)
    g_ckv = sum_model(weight_grad(d_kv, enc_all))

    g_cross = jnp.stack([weight_grad(dq_cross, n2), weight_grad(o_cross, dy_cross)])
    g_cross = g_cross.reshape(2, tp, 2, HEAD_DIM, model)
    g_cross = pick(g_cross, y, 2) + swap_y(pick(g_cross, 1 - y, 2).astype(BF16)).astype(F32)
    g_cross = sum_tp(sum_model(g_cross).transpose(1, 0, 2, 3))
    g_cross = jnp.concatenate([g_ckv.reshape(2, HEAD_DIM, local), g_cross]).astype(BF16)
    g_cross = lax.all_gather(g_cross, "ctx", axis=1, tiled=True).astype(F32)

    dy_self = chip_rows(grad1.astype(BF16))
    do_chip = onto(dy_self, h_out).astype(BF16)
    do_parts = in_order(
        do_chip.reshape(seqs, 2, rows, span, 2, 2 * HEAD_DIM)
        .transpose(0, 3, 4, 1, 2, 5)
        .reshape(tp, 2, 2, rows, 2 * HEAD_DIM),
        tp - z,
    )
    do_parts = jnp.stack(
        [pick(do_parts, y, 1), swap_y(pick(do_parts, 1 - y, 1))], 1
    )
    do_self = jnp.stack(
        [do_parts[0]] + [from_tp(do_parts[tp - e], e) for e in range(1, tp)]
    )
    do_self = do_self.transpose(2, 1, 0, 3, 4).reshape(o_self.shape)
    d_qkv = self_attend_back(qkv, o_self, lse_self, do_self, order)
    d_parts = d_qkv.reshape(4, tp, rows, -1)
    d_n1 = [back_onto(d_parts[g], h_qkv) for g in range(4)]
    d_near, d_far = (
        d_n1[g] + swap_core(d_n1[g + 2].astype(BF16)).astype(F32) for g in range(2)
    )
    d_mine = [
        d_near[e] + swap_y(d_far[e].astype(BF16)).astype(F32) for e in range(tp)
    ]
    came = [d_mine[0]] + [
        from_tp(d_mine[tp - e].astype(BF16), e).astype(F32) for e in range(1, tp)
    ]
    d_n1 = jnp.stack(
        [
            sum(jnp.where(((z + e) % tp) // span == s, came[e], 0.0) for e in range(tp))
            for s in range(seqs)
        ]
    )
    back_self, grad_gain_self, grad_shift_self = layer_norm_back(hidden0, gain_self, d_n1)
    grad_tokens = grad1 + back_self

    g_out = weight_grad(o_chip, dy_self)
    g_out = g_out.reshape(span, 2, 2, HEAD_DIM, model).transpose(1, 2, 0, 3, 4)
    g_out = g_out.reshape(2, tp, HEAD_DIM, model)
    g_out = pick(g_out, y, 0) + swap_y(pick(g_out, 1 - y, 0).astype(BF16)).astype(F32)
    g_out = sum_tp(in_order(sum_model(g_out), tp - z))

    g_qkv = sum(weight_grad(d_parts[g], n1_all[g]) for g in range(4))
    g_qkv = sum_model(g_qkv).reshape(3, 2, HEAD_DIM, local)
    upper = (z >= span).astype(jnp.int32)
    g_qkv = pick(g_qkv, upper, 1) + from_tp(pick(g_qkv, 1 - upper, 1).astype(BF16), span).astype(
        F32
    )
    g_self = jnp.concatenate([g_qkv, g_out[None]]).astype(BF16)
    g_self = lax.all_gather(g_self, "ctx", axis=1, tiled=True).astype(F32)

    sums = lax.psum(
        (grad_gain_cross, grad_shift_cross, grad_gain_ffn, grad_shift_ffn), ("fsdp", "ctx", "tp")
    )
    grad_gain_self, grad_shift_self = lax.psum(
        (grad_gain_self, grad_shift_self), ("fsdp", "ctx", "tp")
    )
    return (
        out_tokens,
        grad_tokens,
        grad_enc,
        grad_gain_self,
        grad_shift_self,
        g_self[0].T,
        g_self[1].T,
        g_self[2].T,
        g_self[3],
        sums[0],
        sums[1],
        g_cross[2].T,
        g_cross[0].T,
        g_cross[1].T,
        g_cross[3],
        sums[2],
        sums[3],
        grad_inner,
        grad_outer,
    )


def solution(mesh):
    in_specs = (
        P("fsdp", ("ctx", "tp"), None),
        P("fsdp", ("ctx", "tp"), None),
        P("fsdp"),
        P("fsdp", ("ctx", "tp"), None),
        P(),
        P(),
        P("fsdp", "tp"),
        P("fsdp", "tp"),
        P("fsdp", "tp"),
        P("tp", "fsdp"),
        P(),
        P(),
        P("fsdp", "tp"),
        P("fsdp", "tp"),
        P("fsdp", "tp"),
        P("tp", "fsdp"),
        P(),
        P(),
        P("fsdp", "tp"),
        P("tp", "fsdp"),
    )
    out_specs = (
        P("fsdp", ("ctx", "tp"), None),
        P("fsdp", ("ctx", "tp"), None),
        P("fsdp", ("ctx", "tp"), None),
        P(),
        P(),
        P("fsdp", "tp"),
        P("fsdp", "tp"),
        P("fsdp", "tp"),
        P("tp", "fsdp"),
        P(),
        P(),
        P("fsdp", "tp"),
        P("fsdp", "tp"),
        P("fsdp", "tp"),
        P("tp", "fsdp"),
        P(),
        P(),
        P("fsdp", "tp"),
        P("tp", "fsdp"),
    )
    return jax.shard_map(shards, mesh=mesh, in_specs=in_specs, out_specs=out_specs, check_vma=False)
```

```python
import functools

import jax
import jax.numpy as jnp
from jax import lax
from jax.experimental import pallas as pl
from jax.experimental.pallas import tpu as pltpu
from jax.sharding import PartitionSpec as P

HEAD_DIM = 64
SCALE = HEAD_DIM ** (-0.5)
BLOCK = 512
MASKED = -1e30
EPS = 1e-05
F32 = jnp.float32
BF16 = jnp.bfloat16
NT = (((1,), (1,)), ((), ()))
NN = (((1,), (0,)), ((), ()))
TN = (((0,), (0,)), ((), ()))


def dot(left, right, dims, precision=None):
    return lax.dot_general(left, right, dims, preferred_element_type=F32, precision=precision)


def shape(dims, dtype):
    return jax.ShapeDtypeStruct(tuple(dims), dtype)


def kernel_call(body, name, scalars, arrays, outs, scratch=(), flops=0):
    vmem = pl.BlockSpec(memory_space=pltpu.VMEM)
    smem = pl.BlockSpec(memory_space=pltpu.SMEM)
    moved = sum(a.size * a.dtype.itemsize for a in arrays)
    moved += sum(a.size * a.dtype.itemsize for a in outs)
    return pl.pallas_call(
        body,
        out_shape=tuple(outs),
        in_specs=[smem] * len(scalars) + [vmem] * len(arrays),
        out_specs=(vmem,) * len(outs),
        scratch_shapes=list(scratch),
        compiler_params=pltpu.CompilerParams(vmem_limit_bytes=56 << 20),
        cost_estimate=pl.CostEstimate(flops=flops // 1, bytes_accessed=moved // 1, transcendentals=0),
        name=name,
    )(*scalars, *arrays)


def span_of(at, i, parts):
    width = parts[i].shape[-1]
    return pl.ds(pl.multiple_of(at[i], 128), width) if len(parts) > 1 else slice(0, width)


def onto(read, parts, at, rows_of=lambda part: part[...]):
    return sum(
        dot(read(span_of(at, i, parts)), rows_of(part), NT) for i, part in enumerate(parts)
    )


def lanes_of(h, width=128):
    return (lax.broadcasted_iota(jnp.int32, (1, width), 1) < width // 2) == (h == 0)


def head(value, h):
    return jnp.where(lanes_of(h), value, jnp.zeros_like(value))


def normal(hidden, gain, shift):
    centre = hidden - jnp.mean(hidden, axis=-1, keepdims=True)
    spread = jnp.mean(centre * centre, axis=-1, keepdims=True)
    return centre * lax.rsqrt(spread + EPS) * gain + shift


def first_norm_kernel(tp, picks, tokens, enc, gain, shift, *rest):
    outs, keep = rest[:tp], rest[tp]
    rows, slots = tokens.shape[1], enc.shape[1]
    for s in range(tokens.shape[0]):
        keep[s] = normal(tokens[s].astype(F32), gain[...], shift[...]).astype(BF16)
    for e in range(tp):
        outs[e][:rows] = keep[picks[e]]
        for s in range(enc.shape[0]):
            outs[e][rows + s * slots : rows + (s + 1) * slots] = enc[s]


def norm_kernel(before, own, got, gain, shift, hidden, normed):
    for s in range(before.shape[0]):
        value = before[s].astype(F32) + own[s] + got[s].astype(F32)
        hidden[s] = value
        normed[s] = normal(value, gain[...], shift[...]).astype(BF16)


def norm_back_rows(hidden, gain, grad):
    centre = hidden - jnp.mean(hidden, axis=-1, keepdims=True)
    rate = lax.rsqrt(jnp.mean(centre * centre, axis=-1, keepdims=True) + EPS)
    unit, scaled = centre * rate, grad * gain
    back = rate * (
        scaled
        - jnp.mean(scaled, axis=-1, keepdims=True)
        - unit * jnp.mean(scaled * unit, axis=-1, keepdims=True)
    )
    return back, jnp.sum(grad * unit, axis=0, keepdims=True), jnp.sum(grad, axis=0, keepdims=True)


def norm_back_kernel(hidden, gain, after, own, *rest):
    got, (grad_out, rounded, sums) = rest[:-3], rest[-3:]
    gains = shifts = None
    for s in range(hidden.shape[0]):
        grad = own[s]
        for more in got:
            grad = grad + more[s].astype(F32)
        back, g, b = norm_back_rows(hidden[s], gain[...], grad)
        gains, shifts = (g, b) if gains is None else (gains + g, shifts + b)
        total = after[s].astype(F32) + back
        grad_out[s] = total
        rounded[s] = total.astype(BF16)
    sums[0:1, :] = gains
    sums[1:2, :] = shifts


def last_norm_kernel(seq_of, tokens, gain, after, own, other, grad_out, acc):
    acc[seq_of[0]] = own[...]
    acc[1 - seq_of[0]] = other[...].astype(F32)
    for s in range(tokens.shape[0]):
        back, _, _ = norm_back_rows(tokens[s].astype(F32), gain[...], acc[s])
        grad_out[s] = after[s] + back


def self_kernel(n_parts, tp, block, at, places, order, *refs):
    groups, refs = refs[:4], refs[4:]
    weights, refs = refs[:n_parts], refs[n_parts:]
    qkv, lse, outs, out_s = refs[0], refs[1], refs[2:-1], refs[-1]
    rows, width = out_s.shape[1], qkv.shape[2]
    length = qkv.shape[1]
    for g in range(4):
        group = groups[g]
        value = onto(
            lambda span: group[:, :rows, span].reshape(tp * rows, -1),
            weights,
            at,
            lambda part: part[0 : 3 * width],
        ).astype(BF16)
        for e in range(tp):
            row = pl.ds(pl.multiple_of(places[g * tp + e] * rows, rows), rows)
            for i in range(3):
                qkv[i, row, :] = value[e * rows : (e + 1) * rows, i * width : (i + 1) * width]
    row = lax.broadcasted_iota(jnp.int32, (block, block), 0)
    col = lax.broadcasted_iota(jnp.int32, (block, block), 1)
    for i in range(length // block):
        first, here = i * block, slice(i * block, (i + 1) * block)
        q = qkv[0, here, :]
        mixed = []
        for h in range(2):
            qh = head(q, h)
            near = jnp.where(row >= col, dot(qh, qkv[1, here, :], NT) * SCALE, MASKED)
            top = jnp.max(near, axis=1, keepdims=True)
            if first:
                far = dot(qh, qkv[1, 0:first, :], NT) * SCALE
                top = jnp.maximum(top, jnp.max(far, axis=1, keepdims=True))
                far = jnp.exp(far - top)
            near = jnp.exp(near - top)
            total = jnp.sum(near, axis=1, keepdims=True)
            acc = dot(near.astype(BF16), qkv[2, here, :], NN)
            if first:
                total = total + jnp.sum(far, axis=1, keepdims=True)
                acc = acc + dot(far.astype(BF16), qkv[2, 0:first, :], NN)
            mixed.append(acc / total)
            flat = jnp.broadcast_to(top + jnp.log(total), (block, 128)).T
            lse[h : h + 1, here] = flat[0:1, :]
        both = jnp.where(lanes_of(0), mixed[0], mixed[1]).astype(BF16)
        for t in range(block // rows):
            out_s[order[i * (block // rows) + t]] = both[t * rows : (t + 1) * rows, :]
    for kr in range(2):
        for j in range(2 * tp):
            outs[j][kr] = out_s[kr * 2 * tp + j]


def cut(ref, i):
    width = ref.shape[-1]
    return slice(i * width, (i + 1) * width)


def pair_rows(pack, i, t_of, tp, e):
    own, mate = t_of[e], t_of[e ^ (tp // 2)]
    return jnp.concatenate(
        [pack[i, own, 0:64], pack[i, mate, 0:64], pack[i, own, 64:128], pack[i, mate, 64:128]],
        axis=0,
    )


def out_kernel(tp, t_of, seq_of, *refs):
    came, refs = refs[: 2 * tp], refs[2 * tp :]
    pack, own, send, acc = refs
    rows = own.shape[1]
    own[...] = jnp.zeros_like(own)
    acc[...] = jnp.zeros_like(acc)
    for e in range(tp):
        value = jnp.concatenate(
            [came[ys * tp + e][...].reshape(2 * rows, -1) for ys in range(2)], axis=1
        )
        s = seq_of[e]
        for i in range(pack.shape[0]):
            span = cut(pack, i)
            got = dot(value, pair_rows(pack, i, t_of, tp, e), NN)
            own[s, :, span] += got[:rows]
            acc[s, :, span] += got[rows:]
    send[...] = acc[...].astype(BF16)


def grad_mixed_kernel(tp, t_of, seq_of, own, got, pack, *outs):
    rows = own.shape[1]
    for e in range(tp):
        s, value = seq_of[e], 0.0
        for i in range(pack.shape[0]):
            span = cut(pack, i)
            left = jnp.concatenate([own[s, :, span], got[s, :, span]], axis=0)
            value = value + dot(left, pair_rows(pack, i, t_of, tp, e), NT)
        value = value.astype(BF16)
        for ys in range(2):
            for kr in range(2):
                outs[ys * tp + e][kr] = value[
                    kr * rows : (kr + 1) * rows, ys * 128 : (ys + 1) * 128
                ]


def chip_rows(own, got, span):
    seqs, rows = own.shape[0], own.shape[1]
    return jnp.concatenate(
        [own[:, :, span].reshape(seqs * rows, -1), got[:, :, span].reshape(seqs * rows, -1)],
        axis=0,
    )


def seq_rows(ref, e, s, seqs, rows):
    return jnp.concatenate(
        [ref[e, (j * seqs + s) * rows : (j * seqs + s + 1) * rows, :] for j in range(2)], axis=0
    )


def keys_values(kv_own, kv_far, e, s, keys):
    part = slice(s * keys, (s + 1) * keys)
    return (
        jnp.concatenate([kv_own[e, 0:64, part], kv_far[e, 0:64, part]], axis=0),
        jnp.concatenate([kv_own[e, 64:128, part], kv_far[e, 64:128, part]], axis=0),
    )


def pair_of(pack, i, t, j):
    return pack[i, t, j * 128 : (j + 1) * 128]


def by_pair(own, got, pack, t, j):
    return sum(
        dot(chip_rows(own, got, cut(pack, i)), pair_of(pack, i, t, j), NT)
        for i in range(pack.shape[0])
    ).astype(BF16)


def pairs_back(value, pack, t_of, j, own, send):
    seqs, rows = own.shape[0], own.shape[1]
    half = seqs * rows
    for i in range(pack.shape[0]):
        span = cut(pack, i)
        total = sum(
            dot(value[e], pair_of(pack, i, t_of[e], j), NN) for e in range(value.shape[0])
        )
        own[:, :, span] = total[:half].reshape(seqs, rows, -1)
        send[:, :, span] = total[half:].astype(BF16).reshape(seqs, rows, -1)


def keys_kernel(n_parts, tp, at, places, *refs):
    groups, refs = refs[:4], refs[4:]
    weights, (enc_all, kv) = refs[:n_parts], refs[n_parts:]
    seqs, keys = enc_all.shape[0], enc_all.shape[1]
    slots = keys // (4 * tp)
    rows = groups[0].shape[1] - seqs * slots
    for g in range(4):
        for e in range(tp):
            row = pl.ds(pl.multiple_of(places[g * tp + e] * slots, slots), slots)
            for s in range(seqs):
                enc_all[s, row, :] = groups[g][e, rows + s * slots : rows + (s + 1) * slots]
    for s in range(seqs):
        total = 0.0
        for i in range(n_parts):
            span = span_of(at, i, weights)
            total = total + dot(weights[i][-kv.shape[0] :], enc_all[s, :, span], NT)
        kv[:, s * keys : (s + 1) * keys] = total.astype(BF16)


def cross_kernel(tp, lengths, t_of, own_in, got_in, kv_own, kv_far, pack, own, send, q_out, o_out, lse):
    seqs, rows = own.shape[0], own.shape[1]
    keys = kv_own.shape[2] // seqs
    for e in range(tp):
        q_out[e] = by_pair(own_in, got_in, pack, t_of[e], 1)
    col = lax.broadcasted_iota(jnp.int32, (2 * rows, keys), 1)
    for s in range(seqs):
        valid = col < lengths[s]
        for e in range(tp):
            q = seq_rows(q_out, e, s, seqs, rows)
            keys_in, values_in = keys_values(kv_own, kv_far, e, s, keys)
            mixed = []
            for h in range(2):
                scores = jnp.where(valid, dot(head(q, h), keys_in, NN) * SCALE, MASKED)
                top = jnp.max(scores, axis=1, keepdims=True)
                probs = jnp.exp(scores - top)
                total = jnp.sum(probs, axis=1, keepdims=True)
                mixed.append(dot(probs.astype(BF16), values_in, NT) / total)
                flat = jnp.broadcast_to(top + jnp.log(total), (2 * rows, 128)).T
                row = (s * tp + e) * 2 + h
                lse[row : row + 1, :] = flat[0:1, :]
            both = jnp.where(lanes_of(0), mixed[0], mixed[1]).astype(BF16)
            for j in range(2):
                o_out[e, (j * seqs + s) * rows : (j * seqs + s + 1) * rows, :] = both[
                    j * rows : (j + 1) * rows
                ]
    pairs_back(o_out, pack, t_of, 2, own, send)


def cross_back_kernel(tp, lengths, t_of, own_in, got_in, q_in, lse, kv_own, kv_far, pack, *refs):
    own, send, dq_out, dkv_own, dkv_far, do_s = refs
    seqs, rows = own.shape[0], own.shape[1]
    keys = kv_own.shape[2] // seqs
    for e in range(tp):
        do_s[e] = by_pair(own_in, got_in, pack, t_of[e], 2)
    key = lax.broadcasted_iota(jnp.int32, (keys, 2 * rows), 0)
    for s in range(seqs):
        valid = key < lengths[s]
        for e in range(tp):
            q, g = seq_rows(q_in, e, s, seqs, rows), seq_rows(do_s, e, s, seqs, rows)
            keys_in, values_in = (v.T for v in keys_values(kv_own, kv_far, e, s, keys))
            dks, dvs, dq = [], [], 0.0
            for h in range(2):
                kh, vh = head(keys_in, h), head(values_in, h)
                row = (s * tp + e) * 2 + h
                scores = dot(kh, q, NT) * SCALE - lse[row : row + 1, :]
                probs = jnp.exp(jnp.where(valid, scores, MASKED))
                dp = dot(vh, g, NT)
                ds = (probs * (dp - jnp.sum(probs * dp, axis=0, keepdims=True))).astype(BF16)
                dvs.append(dot(probs.astype(BF16), g, NN)[:, h * 64 : (h + 1) * 64])
                dks.append(dot(ds, q, NN)[:, h * 64 : (h + 1) * 64] * SCALE)
                dq = dq + dot(ds, kh, TN)
            dq = (dq * SCALE).astype(BF16)
            for j in range(2):
                dq_out[e, (j * seqs + s) * rows : (j * seqs + s + 1) * rows, :] = dq[
                    j * rows : (j + 1) * rows
                ]
            part = slice(s * keys, (s + 1) * keys)
            dkv_own[e, :, part] = jnp.concatenate([dks[0], dvs[0]], axis=1).T.astype(BF16)
            dkv_far[e, :, part] = jnp.concatenate([dks[1], dvs[1]], axis=1).T.astype(BF16)
    pairs_back(dq_out, pack, t_of, 1, own, send)


def ffn_kernel(tp, n_own, n_got, y_own, y_got, weights, *refs):
    active, d_inner, d_own, d_send, o_own, o_send = refs
    seqs, rows = n_own.shape[0], n_own.shape[1]
    half, parts, width = seqs * rows, weights.shape[0], weights.shape[4]
    spans = [slice(i * width, (i + 1) * width) for i in range(parts)]
    for e in range(tp):
        inner = sum(
            dot(chip_rows(n_own, n_got, spans[i]), weights[i, e, 0], NT) for i in range(parts)
        )
        grad = sum(
            dot(chip_rows(y_own, y_got, spans[i]), weights[i, e, 1], NT) for i in range(parts)
        )
        square = inner * inner
        bend = jnp.tanh(0.7978845608 * (inner + 0.044715 * square * inner))
        active[e] = (0.5 * inner * (1.0 + bend)).astype(BF16)
        slope = 0.5 * (1.0 + bend) + 0.5 * inner * (1.0 - bend * bend) * (
            0.7978845608 * (1.0 + 3.0 * 0.044715 * square)
        )
        d_inner[e] = (grad * slope).astype(BF16)
    for j, (out, send, rows_in) in enumerate(((d_own, d_send, d_inner), (o_own, o_send, active))):
        for i in range(parts):
            total = sum(dot(rows_in[e], weights[i, e, j], NN) for e in range(tp))
            out[:, :, spans[i]] = total[:half].reshape(seqs, rows, -1)
            send[:, :, spans[i]] = total[half:].astype(BF16).reshape(seqs, rows, -1)


def ffn_grad_kernel(tp, d_near, d_far, a_near, a_far, *refs):
    n_rows, y_rows, out = refs[:4], refs[4:8], refs[8]
    parts, width = out.shape[0], out.shape[4]
    for j, (near, far, given) in enumerate(
        ((d_near, d_far, n_rows), (a_near, a_far, y_rows))
    ):
        for i in range(parts):
            span = slice(i * width, (i + 1) * width)
            first, second = chip_rows(given[0], given[1], span), chip_rows(given[2], given[3], span)
            for e in range(tp):
                out[i, e, j] = (dot(near[e], first, TN) + dot(far[e], second, TN)).astype(BF16)


def cross_grad_kernel(tp, dq, o, n_own, n_got, y_own, y_got, dkv_far, keep, send):
    parts, width = keep.shape[1], keep.shape[4]
    for j, (left, a, b) in enumerate(((dq, n_own, n_got), (o, y_own, y_got))):
        right = chip_rows(a, b, slice(None))
        for e in range(tp):
            got = dot(left[e], right, TN)
            for i in range(parts):
                span = slice(i * width, (i + 1) * width)
                keep[e, i, j] = got[0:64, span]
                send[e, (2 * i + j) * 64 : (2 * i + j + 1) * 64] = got[64:128, span].astype(BF16)
    send[:, 2 * parts * 64 :] = dkv_far[...]


def out_grad_kernel(tp, seq_of, own, got, *refs):
    came, (keep, send, acc) = refs[: 2 * tp], refs[2 * tp :]
    rows = own.shape[1]
    acc[...] = jnp.zeros_like(acc)
    for e in range(tp):
        s, mate = seq_of[e], e ^ (tp // 2)
        right = jnp.concatenate([own[s], got[s]], axis=0)
        for ys in range(2):
            left = came[ys * tp + e][...].reshape(2 * rows, -1)
            value = dot(left, right, TN)
            acc[ys, e] += value[0:64]
            acc[ys, mate] += value[64:128]
    keep[...] = acc[0]
    send[...] = acc[1].astype(BF16)


def enc_grad_kernel(n_parts, tp, at, places, d_kv, enc_all, *refs):
    weights, (keep, send, grad_w, all_s) = refs[:n_parts], refs[n_parts:]
    seqs, keys, model = enc_all.shape
    slots = keys // (4 * tp)
    total = 0.0
    for s in range(seqs):
        part = d_kv[:, s * keys : (s + 1) * keys]
        total = total + dot(part, enc_all[s], NN)
        for i in range(n_parts):
            all_s[s, :, span_of(at, i, weights)] = dot(part, weights[i][-d_kv.shape[0] :], TN)
    grad_w[...] = total
    for g in range(4):
        for e in range(tp):
            row = pl.ds(pl.multiple_of(places[g * tp + e] * slots, slots), slots)
            for s in range(seqs):
                if g < 2:
                    keep[g, e, s] = all_s[s, row, :]
                else:
                    send[g - 2, e, s] = all_s[s, row, :].astype(BF16)


def turn_kernel(count, offsets, *refs):
    pieces, outs = refs[:4], refs[4:-1]
    all_s = refs[-1]
    for j, out in enumerate(outs):
        part = pieces[0].shape[1]
        for i in range(4):
            all_s[pl.ds(pl.multiple_of(offsets[i] * part, part), part), :] = pieces[i][j].astype(F32)
        out[...] = all_s[...].T if j < count else all_s[...]


def qkv_grad_kernel(n_parts, tp, at, grads, *refs):
    groups, refs = refs[:4], refs[4:]
    weights, outs, sums = refs[:n_parts], refs[n_parts:-1], refs[-1]
    rows, columns = grads.shape[1], grads.shape[2]
    left = [grads[g * tp : (g + 1) * tp].reshape(-1, columns) for g in range(4)]
    ones = jnp.ones((8, left[0].shape[0]), BF16)
    counts = sum(dot(ones, part, NN) for part in left)
    for i in range(n_parts):
        span = span_of(at, i, outs)
        total = 0.0
        for g in range(4):
            right = groups[g][:, :rows, span].reshape(left[g].shape[0], -1)
            total = total + dot(left[g], right, TN)
        outs[i][...] = total.astype(outs[i].dtype)
        weight = weights[i][0:columns].astype(F32)
        sums[0:1, span] = jnp.sum(total * weight, axis=0, keepdims=True)
        sums[1:2, span] = dot(counts, weight, NN, lax.Precision.HIGHEST)[0:1]


def self_back_kernel(n_parts, tp, block, at, order, qkv, lse, *refs):
    outs, grads, refs = refs[: 2 * tp], refs[2 * tp : 4 * tp], refs[4 * tp :]
    weights, (grad_qkv, keep, send, g_s, sum_s, dq_s) = refs[:n_parts], refs[n_parts:]
    length, width = qkv.shape[1], qkv.shape[2]
    rows = outs[0].shape[1]
    lane8 = lax.broadcasted_iota(jnp.int32, (8, width), 1)
    row8 = lax.broadcasted_iota(jnp.int32, (8, width), 0)
    chosen = jnp.where(lane8 // (width // 2) == row8, 1.0, 0.0).astype(F32)
    for j in range(2 * tp):
        for kr in range(2):
            r = kr * 2 * tp + j
            here = pl.ds(pl.multiple_of(order[r] * rows, rows), rows)
            g_s[here, :] = grads[j][kr]
            sum_s[:, here] = dot(
                chosen,
                grads[j][kr].astype(F32) * outs[j][kr].astype(F32),
                NT,
                lax.Precision.HIGHEST,
            )
    row = lax.broadcasted_iota(jnp.int32, (block, block), 0)
    col = lax.broadcasted_iota(jnp.int32, (block, block), 1)
    dq_s[...] = jnp.zeros_like(dq_s)
    blocks = length // block
    for j in range(blocks):
        here = slice(j * block, (j + 1) * block)
        kj, vj = qkv[1, here, :], qkv[2, here, :]
        dks, dvs = [], []
        for h in range(2):
            kh, vh = head(kj, h), head(vj, h)
            dk = dv = 0.0
            for i in range(j, blocks):
                there = slice(i * block, (i + 1) * block)
                q, g = qkv[0, there, :], g_s[there, :]
                scores = dot(kh, q, NT) * SCALE - lse[h : h + 1, there]
                if i == j:
                    scores = jnp.where(col >= row, scores, MASKED)
                probs = jnp.exp(scores)
                ds = (probs * (dot(vh, g, NT) - sum_s[h : h + 1, there])).astype(BF16)
                dv, dk = dv + dot(probs.astype(BF16), g, NN), dk + dot(ds, q, NN)
                dq_s[there, :] += dot(ds, kh, TN)
            dks.append(dk)
            dvs.append(dv)
        dk = (jnp.where(lanes_of(0), dks[0], dks[1]) * SCALE).astype(BF16)
        dv = jnp.where(lanes_of(0), dvs[0], dvs[1]).astype(BF16)
        qkv_rows = block // rows
        for t in range(qkv_rows):
            r, part = order[4 * tp + j * qkv_rows + t], slice(t * rows, (t + 1) * rows)
            grad_qkv[r, :, width : 2 * width] = dk[part]
            grad_qkv[r, :, 2 * width : 3 * width] = dv[part]
    for p in range(4 * tp):
        grad_qkv[order[4 * tp + p], :, 0:width] = (
            dq_s[p * rows : (p + 1) * rows, :] * SCALE
        ).astype(BF16)
    for g in (2, 3, 0, 1):
        left = grad_qkv[g * tp : (g + 1) * tp].reshape(tp * rows, -1)
        for i in range(n_parts):
            span = span_of(at, i, weights)
            value = dot(left, weights[i][0 : 3 * width], NN).reshape(tp, rows, -1)
            if g < 2:
                keep[g, :, :, span] = value
            else:
                send[g - 2, :, :, span] = value.astype(BF16)


def swap(value, axis, bit):
    return lax.ppermute(value, axis, [(i, i ^ bit) for i in range(lax.axis_size(axis))])


def swap_core(value):
    return swap(value, "ctx", 1)


def swap_y(value):
    return swap(value, "ctx", 2)


def from_tp(value, step):
    return swap(value, "tp", step)


def from_chip(value, far, step):
    ctx, size = lax.axis_size("ctx"), lax.axis_size("tp")
    if far == 0 and step == 0:
        return value
    pairs = [
        ((c ^ (2 * far)) * size + (i ^ step), c * size + i)
        for c in range(ctx)
        for i in range(size)
    ]
    return lax.ppermute(value, ("ctx", "tp"), pairs)


def after(value, *others):
    return lax.optimization_barrier((value, others))[0]


def pick(value, index, axis):
    return lax.dynamic_index_in_dim(value, index, axis, keepdims=False)


def gather_tp(value):
    return jnp.stack([value] + [from_tp(value, e) for e in range(1, lax.axis_size("tp"))])


def model_parts(value):
    if lax.axis_size("fsdp") == 2:
        return (value, swap(value, "fsdp", 1))
    return (lax.all_gather(value, "fsdp", axis=value.ndim - 1, tiled=True),)


def sum_model(value):
    if lax.axis_size("fsdp") != 2:
        return lax.psum_scatter(
            value.astype(BF16), "fsdp", scatter_dimension=value.ndim - 1, tiled=True
        ).astype(F32)
    width, mine = value.shape[-1] // 2, lax.axis_index("fsdp")
    keep = lax.dynamic_slice_in_dim(value, mine * width, width, value.ndim - 1)
    send = lax.dynamic_slice_in_dim(value, (1 - mine) * width, width, value.ndim - 1)
    return keep.astype(F32) + swap(send.astype(BF16), "fsdp", 1).astype(F32)


def sum_parts(parts):
    if len(parts) == 1:
        return sum_model(parts[0])
    return parts[0].astype(F32) + swap(parts[1], "fsdp", 1).astype(F32)


def sum_tp(pieces):
    total = pieces[0].astype(F32)
    for e in range(1, lax.axis_size("tp")):
        total = total + from_tp(pieces[e].astype(BF16), e).astype(F32)
    return total


def sum_all(value):
    for axis in ("ctx", "tp", "fsdp"):
        if axis == "fsdp" and lax.axis_size(axis) != 2:
            value = lax.psum(value, axis)
            continue
        bit = 1
        while bit < lax.axis_size(axis):
            value = value + swap(value, axis, bit)
            bit *= 2
    return value


def shards(
    tokens,
    enc_states,
    enc_lengths,
    cotangent,
    gain_self,
    shift_self,
    w_query,
    w_key,
    w_value,
    w_out,
    gain_cross,
    shift_cross,
    cross_query,
    cross_key,
    cross_value,
    cross_out,
    gain_ffn,
    shift_ffn,
    w_inner,
    w_outer,
):
    seqs, rows, model = tokens.shape
    tp, ctx = lax.axis_size("tp"), lax.axis_size("ctx")
    z, c = lax.axis_index("tp"), lax.axis_index("ctx")
    y, k = c // 2, c % 2
    span = tp // 2
    local = w_query.shape[0]
    hid = w_inner.shape[1] // ctx
    own_rows = tokens.shape
    chip = 2 * seqs * rows
    n_parts = 2 if lax.axis_size("fsdp") == 2 else 1
    mine = lax.axis_index("fsdp") * local if n_parts == 2 else 0
    at = jnp.stack([jnp.int32(mine), jnp.int32(model // 2 - mine)])
    step = jnp.arange(tp, dtype=jnp.int32)
    seq_of = (z ^ step) // span
    two = lambda vector: vector.reshape(1, -1)
    gains = [two(g) for g in (gain_self, shift_self, gain_cross, shift_cross, gain_ffn, shift_ffn)]

    rel = jnp.arange(4 * tp, dtype=jnp.int32)
    places = (2 * ((rel // tp) % 2 ^ y) + ((rel // (2 * tp)) ^ k)) * tp + ((rel % tp) ^ z)
    order = ((((rel // tp) % 2) ^ k) * 2 + ((rel // (2 * tp)) ^ y)) * tp + ((rel % tp) ^ z)
    places, order = places.astype(jnp.int32), order.astype(jnp.int32)

    def own_head(weight):
        return lax.dynamic_slice_in_dim(weight, c * HEAD_DIM, HEAD_DIM, 0)

    def core_half(weight):
        other = lax.dynamic_slice_in_dim(weight, (c ^ 2) * HEAD_DIM, HEAD_DIM, 0)
        return jnp.concatenate([own_head(weight), other])

    own_qkv = jnp.stack([own_head(w.T) for w in (w_query, w_key, w_value)])
    own_ckv = jnp.concatenate([own_head(cross_key.T), own_head(cross_value.T)])
    own_qkv, picks = lax.optimization_barrier((own_qkv, (z ^ step) // span))
    other_qkv = from_tp(own_qkv, span)
    slots = enc_states.shape[1]
    keys = 4 * tp * slots
    pieces = kernel_call(
        functools.partial(first_norm_kernel, tp),
        "norm_self",
        [picks],
        [tokens, enc_states, gains[0], gains[1]],
        [shape((rows + seqs * slots, model), BF16)] * tp,
        [pltpu.VMEM(own_rows, BF16)],
    )
    t_of = (z ^ step).astype(jnp.int32)
    pack = jnp.concatenate([core_half(w) for w in (w_out, cross_query.T, cross_out)])

    def gather_weights(value):
        got = lax.all_gather(value, ("fsdp", "tp"))
        got = got.reshape(-1, tp, *value.shape)
        if n_parts == 2:
            return got
        return jnp.moveaxis(got, 0, -2).reshape(1, tp, *value.shape[:-1], model)

    which = jnp.stack([c, c ^ 1, c ^ 2, c ^ 3]).astype(jnp.int32)
    near = [pieces[0]] + [None] * (tp - 1)
    bit = span
    while bit:
        for e in range(0, tp, 2 * bit):
            near[e + bit] = from_tp(pieces[bit] if e == 0 else near[e], bit)
        bit //= 2
    far = [swap_y(piece) for piece in near]
    near = jnp.stack(after(near, other_qkv, far[0]))
    h_qkv = model_parts(
        jnp.concatenate([jnp.stack([own_qkv, other_qkv], 1).reshape(-1, local), own_ckv])
    )
    far = after(jnp.stack(far), h_qkv)
    groups = [near, far, swap_core(near), swap_core(far)]

    h_ffn = jnp.stack(
        [
            lax.dynamic_slice_in_dim(w_inner, c * hid, hid, 1).T,
            lax.dynamic_slice_in_dim(w_outer, c * hid, hid, 0),
        ]
    )
    pack = gather_weights(after(pack, near))
    h_ffn = gather_weights(after(h_ffn, near))
    y_far = swap_y(after(cotangent, far))
    y_rows = [cotangent, swap_core(after(cotangent, near)), y_far]

    enc_all, kv_own = kernel_call(
        functools.partial(keys_kernel, n_parts, tp),
        "cross_keys",
        [at, places],
        [*groups, *h_qkv],
        [shape((seqs, keys, model), BF16), shape((2 * HEAD_DIM, seqs * keys), BF16)],
        flops=4 * seqs * keys * model * 2 * HEAD_DIM,
    )
    kv_at = kv_own
    kv_own = gather_tp(kv_own)

    length, width = ctx * tp * rows, 2 * HEAD_DIM
    qkv, lse_self, *o_sent = kernel_call(
        functools.partial(self_kernel, n_parts, tp, BLOCK),
        "self_attend",
        [after(at, kv_at), places, order],
        [*groups, *h_qkv],
        [shape((3, length, width), BF16), shape((2, length), F32)]
        + [shape((2, rows, width), BF16)] * (2 * tp),
        [pltpu.VMEM((4 * tp, rows, width), BF16)],
        flops=4 * length * length * width + 6 * length * model * width,
    )
    o_sent = after(o_sent, kv_own)
    kv_far = swap_y(kv_own)
    came = [
        from_chip(o_sent[ys * tp + e], ys, e) for ys in range(2) for e in range(tp)
    ]
    partial_own, partial_send = kernel_call(
        functools.partial(out_kernel, tp),
        "out_self",
        [t_of, seq_of],
        [*came, pack],
        [shape(own_rows, F32), shape(own_rows, BF16)],
        [pltpu.VMEM(own_rows, F32)],
        flops=2 * chip * 4 * width * model,
    )

    def add_norm(before, own, sent, which):
        return kernel_call(
            norm_kernel,
            "add_norm",
            [],
            [before, own, swap_core(sent), gains[2 * which], gains[2 * which + 1]],
            [shape(own_rows, F32), shape(own_rows, BF16)],
        )

    hidden1, n2 = add_norm(tokens, partial_own, partial_send, 1)

    n2_got = swap_core(n2)
    partial_own, partial_send, q_cross, o_cross, lse_cross = kernel_call(
        functools.partial(cross_kernel, tp),
        "cross_attend",
        [enc_lengths, after(t_of, y_far)],
        [n2, n2_got, kv_own, kv_far, pack],
        [
            shape(own_rows, F32),
            shape(own_rows, BF16),
            shape((tp, chip, width), BF16),
            shape((tp, chip, width), BF16),
            shape((seqs * tp * 2, 2 * rows), F32),
        ],
        flops=4 * chip * tp * width * (model + keys),
    )
    hidden2, n3 = add_norm(hidden1, partial_own, partial_send, 2)

    n3_far = swap_y(n3)
    y_rows.append(swap_core(after(y_far, n3)))
    n_rows = [n3, swap_core(n3), n3_far, swap_core(n3_far)]

    def feed(first):
        return kernel_call(
            functools.partial(ffn_kernel, tp),
            "feed_forward",
            [],
            [*n_rows[first : first + 2], *y_rows[first : first + 2], h_ffn],
            [shape((tp, chip, hid), BF16)] * 2 + [shape(own_rows, F32), shape(own_rows, BF16)] * 2,
            flops=8 * chip * model * tp * hid,
        )

    a_far, d_far, dn_far, dn_far_send, out_far, out_far_send = feed(2)
    a_near, d_near, dn_own, dn_near_send, out_own, out_near_send = feed(0)

    def far_sum(own, sent):
        return (own + swap_core(sent).astype(F32)).astype(BF16)

    dn_near = swap_core(dn_near_send)
    dn_far = far_sum(dn_far, dn_far_send)
    g_ffn = kernel_call(
        functools.partial(ffn_grad_kernel, tp),
        "grad_feed_forward",
        [],
        [after(d_near, dn_far, dn_near), d_far, a_near, a_far, *n_rows, *y_rows],
        [shape((n_parts, tp, 2, hid, model // n_parts), BF16)],
        flops=8 * chip * model * tp * hid,
    )[0]
    dn_far = swap_y(dn_far)

    def norm_back(hidden, gain, before, own, *got):
        return kernel_call(
            norm_back_kernel,
            "norm_back",
            [],
            [hidden, gain, before, own, *got],
            [shape(own_rows, F32), shape(own_rows, BF16), shape((2, model), F32)],
        )

    grad2, y2, sums_ffn = norm_back(
        hidden2, after(gains[4], g_ffn), cotangent, dn_own, dn_near, dn_far
    )
    if n_parts == 1:
        g_ffn = g_ffn.reshape(tp, 2, hid, -1, local).transpose(3, 0, 1, 2, 4)
    g_ffn = lax.psum_scatter(
        after(g_ffn.reshape(-1, 2, hid, local), y2), ("fsdp", "tp"), scatter_dimension=0
    )
    g_ffn = lax.all_gather(g_ffn.astype(BF16), "ctx", axis=1, tiled=True)

    y2_got = swap_core(y2)
    held, out_near_send, out_far_send = after((out_far, out_near_send, out_far_send), y2)
    out_near, out_far = swap_core(out_near_send), far_sum(held, out_far_send)
    dn_own, dn_send, dq_cross, dkv_own, dkv_far = kernel_call(
        functools.partial(cross_back_kernel, tp),
        "cross_attend_back",
        [enc_lengths, after(t_of, out_near, out_far)],
        [y2, y2_got, q_cross, lse_cross, kv_own, kv_far, pack],
        [
            shape(own_rows, F32),
            shape(own_rows, BF16),
            shape((tp, chip, width), BF16),
            shape(kv_own.shape, BF16),
            shape(kv_own.shape, BF16),
        ],
        [pltpu.VMEM((tp, chip, width), BF16)],
        flops=4 * chip * tp * width * (model + 3 * keys),
    )
    dn_got = swap_core(dn_send)
    half = seqs * keys
    halves = model // half
    keep, send = kernel_call(
        functools.partial(cross_grad_kernel, tp),
        "grad_cross",
        [],
        [dq_cross, o_cross, n2, n2_got, y2, y2_got, dkv_far],
        [
            shape((tp, halves, 2, HEAD_DIM, half), F32),
            shape((tp, 2 * halves * HEAD_DIM + width, half), BF16),
        ],
        flops=4 * chip * tp * width * model,
    )
    cross_got = swap_y(send)
    grad1, y1, sums_cross = norm_back(hidden1, gains[2], grad2, dn_own, dn_got)

    y1_got = swap_core(y1)
    do_sent = kernel_call(
        functools.partial(grad_mixed_kernel, tp),
        "grad_mixed",
        [t_of, seq_of],
        [y1, y1_got, pack],
        [shape((2, rows, width), BF16)] * (2 * tp),
        flops=2 * chip * 4 * width * model,
    )
    do_came = [
        from_chip(do_sent[ys * tp + e], ys, e) for ys in range(2) for e in range(tp)
    ]
    out_keep, out_send = kernel_call(
        functools.partial(out_grad_kernel, tp),
        "grad_out",
        [after(seq_of, do_sent)],
        [y1, y1_got, *came],
        [shape((tp, HEAD_DIM, model), F32), shape((tp, HEAD_DIM, model), BF16)],
        [pltpu.VMEM((2, tp, HEAD_DIM, model), F32)],
        flops=2 * chip * tp * width * model,
    )
    cross_got = after(cross_got, do_came)
    g_cross = keep + cross_got[:, :-width].reshape(keep.shape).astype(F32)
    d_kv = dkv_own.astype(F32) + cross_got[:, -width:].astype(F32)
    first = lax.axis_index("fsdp") if n_parts == 2 else 0
    cross_x = swap(pick(g_cross, 1 - first, 1).astype(BF16), "fsdp", 1) if n_parts == 2 else None
    out_far = swap_y(after(out_far, do_came))
    out_got = swap_y(after(out_send, do_came))
    d_qkv, dn_keep, dn_send = kernel_call(
        functools.partial(self_back_kernel, n_parts, tp, BLOCK),
        "self_attend_back",
        [after(at, out_keep, g_cross), jnp.concatenate([places, order])],
        [qkv, lse_self, *o_sent, *do_came, *h_qkv],
        [
            shape((4 * tp, rows, 3 * width), BF16),
            shape((2, tp, rows, model), F32),
            shape((2, tp, rows, model), BF16),
        ],
        [
            pltpu.VMEM((length, width), BF16),
            pltpu.VMEM((8, length), F32),
            pltpu.VMEM((length, width), F32),
        ],
        flops=10 * length * length * width + 6 * length * model * width,
    )
    dn_send, dn_keep, cross_x, out_got, out_far = after(
        (dn_send, dn_keep, cross_x, out_got, out_far), d_qkv
    )
    dn_got = swap_core(dn_send)
    dn_sent = [(dn_keep[1, e] + dn_got[1, e].astype(F32)).astype(BF16) for e in range(tp)]
    dn_near = [dn_keep[0, e] + dn_got[0, e].astype(F32) for e in range(tp)]
    g_cross, d_kv, cross_x, out_got, out_far = after(
        (g_cross, d_kv, cross_x, out_got, out_far), dn_sent
    )
    dn_upper = swap_y(jnp.stack(dn_sent[span:]))
    dn_lower = swap_y(jnp.stack(dn_sent[:span]))
    if n_parts == 2:
        g_cross = pick(g_cross, first, 1) + cross_x.astype(F32)
        g_cross = sum_tp(jnp.concatenate([g_cross.reshape(tp, -1, local), d_kv], axis=1))
        g_cross = after(g_cross, dn_upper)
        g_cross, d_kv = g_cross[: 2 * HEAD_DIM].reshape(2, HEAD_DIM, local), g_cross[2 * HEAD_DIM :]
    else:
        g_cross = sum_tp(
            sum_model(g_cross.transpose(0, 2, 3, 1, 4).reshape(tp, 2, HEAD_DIM, model))
        )
        d_kv = sum_tp(d_kv)
    out_tokens = (hidden2 + out_own + out_near.astype(F32) + out_far.astype(F32)).astype(BF16)
    grad_inner, grad_outer = after(g_ffn[0], dn_sent).T.astype(F32), g_ffn[1].astype(F32)
    *g_qkv, sums_self = kernel_call(
        functools.partial(qkv_grad_kernel, n_parts, tp),
        "grad_qkv",
        [after(at, dn_sent, grad_inner, grad_outer)],
        [d_qkv, *groups, *h_qkv],
        (
            [shape((3 * width, model), F32)]
            if n_parts == 1
            else [shape((3 * width, local), F32), shape((3 * width, local), BF16)]
        )
        + [shape((2, model), F32)],
        flops=6 * length * width * model,
    )
    enc_keep, enc_send, g_ckv = kernel_call(
        functools.partial(enc_grad_kernel, n_parts, tp),
        "grad_enc",
        [at, places],
        [d_kv.astype(BF16), enc_all, *h_qkv],
        [
            shape((2, tp, seqs, slots, model), F32),
            shape((2, tp, seqs, slots, model), BF16),
            shape((2 * HEAD_DIM, model), F32),
        ],
        [pltpu.VMEM((seqs, keys, model), F32)],
        flops=4 * seqs * keys * width * model,
    )
    enc_got = swap_core(enc_send)
    enc_far = swap_y((enc_keep[1] + enc_got[1].astype(F32)).astype(BF16))
    grad_enc = sum_tp(enc_keep[0] + enc_got[0].astype(F32) + enc_far.astype(F32))
    g_out = sum_model(out_keep + out_got.astype(F32))
    dn_pieces = [dn_near[e] + dn_lower[e].astype(F32) for e in range(span)]
    dn_pieces += [dn_near[span + e] + dn_upper[e].astype(F32) for e in range(span)]
    for first_piece in (span, 0):
        count = span
        while count > 1:
            count //= 2
            for e in range(count):
                got = from_tp(dn_pieces[first_piece + count + e].astype(BF16), count)
                if first_piece:
                    dn_began = got
                dn_pieces[first_piece + e] = dn_pieces[first_piece + e] + got.astype(F32)
    dn_other = from_tp(dn_pieces[span].astype(BF16), span)
    grad_tokens = kernel_call(
        last_norm_kernel,
        "norm_back_self",
        [seq_of],
        [tokens, gains[0], grad1, dn_pieces[0], dn_other],
        [shape(own_rows, F32)],
        [pltpu.VMEM(own_rows, F32)],
    )[0]

    sums = jnp.concatenate([sums_self, sums_cross, sums_ffn])
    sums = sum_all(after(sums, dn_began))
    grad_shift_self = sums[1]
    grad_gain_self = (sums[0] - shift_self * sums[1]) / gain_self

    def turned(pieces, count):
        quarters = pieces[0].shape[0]
        return kernel_call(
            functools.partial(turn_kernel, count),
            "turn",
            [which],
            pieces,
            [
                shape((pieces[0].shape[2], 4 * pieces[0].shape[1])[:: 1 if j < count else -1], F32)
                for j in range(quarters)
            ],
            [pltpu.VMEM((4 * pieces[0].shape[1], pieces[0].shape[2]), F32)],
        )

    def along_ctx(value):
        far = swap_y(value)
        return [value, swap_core(value), far, swap_core(far)]


    g_cross = jnp.concatenate([sum_model(g_ckv).reshape(2, HEAD_DIM, local), g_cross]).astype(BF16)
    g_cross = lax.all_gather(g_cross, "ctx", axis=1, tiled=True).astype(F32)
    g_qkv, g_out = after((sum_parts(g_qkv), g_out), dn_began)
    g_qkv = g_qkv.reshape(3, 2, HEAD_DIM, local)
    total, g_mate = g_out[0], g_qkv[:, 1].reshape(-1, local)
    for e in range(1, tp):
        piece = g_out[e]
        if e == span:
            got = from_tp(jnp.concatenate([piece, g_mate]).astype(BF16), e).astype(F32)
            total, g_mate = total + got[:HEAD_DIM], got[HEAD_DIM:]
        else:
            total = total + from_tp(piece.astype(BF16), e).astype(F32)
    g_qkv = g_qkv[:, 0] + g_mate.reshape(3, HEAD_DIM, local)
    g_self = jnp.concatenate([g_qkv, total[None]]).astype(BF16)
    g_self = turned(along_ctx(g_self), 3)
    return (
        out_tokens,
        grad_tokens,
        grad_enc,
        grad_gain_self,
        grad_shift_self,
        g_self[0],
        g_self[1],
        g_self[2],
        g_self[3],
        sums[2],
        sums[3],
        g_cross[2].T,
        g_cross[0].T,
        g_cross[1].T,
        g_cross[3],
        sums[4],
        sums[5],
        grad_inner,
        grad_outer,
    )


def solution(mesh):
    in_specs = (
        P("fsdp", ("ctx", "tp"), None),
        P("fsdp", ("ctx", "tp"), None),
        P("fsdp"),
        P("fsdp", ("ctx", "tp"), None),
        P(),
        P(),
        P("fsdp", "tp"),
        P("fsdp", "tp"),
        P("fsdp", "tp"),
        P("tp", "fsdp"),
        P(),
        P(),
        P("fsdp", "tp"),
        P("fsdp", "tp"),
        P("fsdp", "tp"),
        P("tp", "fsdp"),
        P(),
        P(),
        P("fsdp", "tp"),
        P("tp", "fsdp"),
    )
    out_specs = (
        P("fsdp", ("ctx", "tp"), None),
        P("fsdp", ("ctx", "tp"), None),
        P("fsdp", ("ctx", "tp"), None),
        P(),
        P(),
        P("fsdp", "tp"),
        P("fsdp", "tp"),
        P("fsdp", "tp"),
        P("tp", "fsdp"),
        P(),
        P(),
        P("fsdp", "tp"),
        P("fsdp", "tp"),
        P("fsdp", "tp"),
        P("tp", "fsdp"),
        P(),
        P(),
        P("fsdp", "tp"),
        P("tp", "fsdp"),
    )
    return jax.shard_map(shards, mesh=mesh, in_specs=in_specs, out_specs=out_specs, check_vma=False)
```

```python
import functools

import jax
import jax.numpy as jnp
from jax import lax
from jax.experimental import pallas as pl
from jax.experimental.pallas import tpu as pltpu
from jax.sharding import PartitionSpec as P

HEAD_DIM = 64
SCALE = HEAD_DIM ** (-0.5)
BLOCK = 512
MASKED = -1e30
EPS = 1e-05
F32 = jnp.float32
BF16 = jnp.bfloat16
NT = (((1,), (1,)), ((), ()))
NN = (((1,), (0,)), ((), ()))
TN = (((0,), (0,)), ((), ()))


def dot(left, right, dims, precision=None):
    return lax.dot_general(left, right, dims, preferred_element_type=F32, precision=precision)


def shape(dims, dtype):
    return jax.ShapeDtypeStruct(tuple(dims), dtype)


def kernel_call(body, name, scalars, arrays, outs, scratch=(), flops=0):
    vmem = pl.BlockSpec(memory_space=pltpu.VMEM)
    smem = pl.BlockSpec(memory_space=pltpu.SMEM)
    moved = sum(a.size * a.dtype.itemsize for a in arrays)
    moved += sum(a.size * a.dtype.itemsize for a in outs)
    return pl.pallas_call(
        body,
        out_shape=tuple(outs),
        in_specs=[smem] * len(scalars) + [vmem] * len(arrays),
        out_specs=(vmem,) * len(outs),
        scratch_shapes=list(scratch),
        compiler_params=pltpu.CompilerParams(vmem_limit_bytes=56 << 20),
        cost_estimate=pl.CostEstimate(flops=flops // 1, bytes_accessed=moved // 1, transcendentals=0),
        name=name,
    )(*scalars, *arrays)


def span_of(at, i, parts):
    width = parts[i].shape[-1]
    return pl.ds(pl.multiple_of(at[i], 128), width) if len(parts) > 1 else slice(0, width)


def onto(read, parts, at, rows_of=lambda part: part[...]):
    return sum(
        dot(read(span_of(at, i, parts)), rows_of(part), NT) for i, part in enumerate(parts)
    )


def lanes_of(h, width=128):
    return (lax.broadcasted_iota(jnp.int32, (1, width), 1) < width // 2) == (h == 0)


def head(value, h):
    return jnp.where(lanes_of(h), value, jnp.zeros_like(value))


def normal(hidden, gain, shift):
    centre = hidden - jnp.mean(hidden, axis=-1, keepdims=True)
    spread = jnp.mean(centre * centre, axis=-1, keepdims=True)
    return centre * lax.rsqrt(spread + EPS) * gain + shift


def first_norm_kernel(tp, picks, tokens, enc, gain, shift, *rest):
    outs, keep = rest[:tp], rest[tp]
    rows, slots = tokens.shape[1], enc.shape[1]
    for s in range(tokens.shape[0]):
        keep[s] = normal(tokens[s].astype(F32), gain[...], shift[...]).astype(BF16)
    for e in range(tp):
        outs[e][:rows] = keep[picks[e]]
        for s in range(enc.shape[0]):
            outs[e][rows + s * slots : rows + (s + 1) * slots] = enc[s]


def norm_kernel(before, own, got, gain, shift, hidden, normed):
    for s in range(before.shape[0]):
        value = before[s].astype(F32) + own[s] + got[s].astype(F32)
        hidden[s] = value
        normed[s] = normal(value, gain[...], shift[...]).astype(BF16)


def norm_back_rows(hidden, gain, grad):
    centre = hidden - jnp.mean(hidden, axis=-1, keepdims=True)
    rate = lax.rsqrt(jnp.mean(centre * centre, axis=-1, keepdims=True) + EPS)
    unit, scaled = centre * rate, grad * gain
    back = rate * (
        scaled
        - jnp.mean(scaled, axis=-1, keepdims=True)
        - unit * jnp.mean(scaled * unit, axis=-1, keepdims=True)
    )
    return back, jnp.sum(grad * unit, axis=0, keepdims=True), jnp.sum(grad, axis=0, keepdims=True)


def norm_back_kernel(hidden, gain, after, own, *rest):
    got, (grad_out, rounded, sums) = rest[:-3], rest[-3:]
    gains = shifts = None
    for s in range(hidden.shape[0]):
        grad = own[s]
        for more in got:
            grad = grad + more[s].astype(F32)
        back, g, b = norm_back_rows(hidden[s], gain[...], grad)
        gains, shifts = (g, b) if gains is None else (gains + g, shifts + b)
        total = after[s].astype(F32) + back
        grad_out[s] = total
        rounded[s] = total.astype(BF16)
    sums[0:1, :] = gains
    sums[1:2, :] = shifts


def last_norm_kernel(seq_of, tokens, gain, after, own, other, grad_out, acc):
    acc[seq_of[0]] = own[...]
    acc[1 - seq_of[0]] = other[...].astype(F32)
    for s in range(tokens.shape[0]):
        back, _, _ = norm_back_rows(tokens[s].astype(F32), gain[...], acc[s])
        grad_out[s] = after[s] + back


def self_kernel(n_parts, tp, block, at, places, order, *refs):
    groups, refs = refs[:4], refs[4:]
    weights, refs = refs[:n_parts], refs[n_parts:]
    qkv, lse, outs, out_s = refs[0], refs[1], refs[2:-1], refs[-1]
    rows, width = out_s.shape[1], qkv.shape[2]
    length = qkv.shape[1]
    for g in range(4):
        group = groups[g]
        value = onto(
            lambda span: group[:, :rows, span].reshape(tp * rows, -1),
            weights,
            at,
            lambda part: part[0 : 3 * width],
        ).astype(BF16)
        for e in range(tp):
            row = pl.ds(pl.multiple_of(places[g * tp + e] * rows, rows), rows)
            for i in range(3):
                qkv[i, row, :] = value[e * rows : (e + 1) * rows, i * width : (i + 1) * width]
    row = lax.broadcasted_iota(jnp.int32, (block, block), 0)
    col = lax.broadcasted_iota(jnp.int32, (block, block), 1)
    for i in range(length // block):
        first, here = i * block, slice(i * block, (i + 1) * block)
        q = qkv[0, here, :]
        mixed = []
        for h in range(2):
            qh = head(q, h)
            near = jnp.where(row >= col, dot(qh, qkv[1, here, :], NT) * SCALE, MASKED)
            top = jnp.max(near, axis=1, keepdims=True)
            if first:
                far = dot(qh, qkv[1, 0:first, :], NT) * SCALE
                top = jnp.maximum(top, jnp.max(far, axis=1, keepdims=True))
                far = jnp.exp(far - top)
            near = jnp.exp(near - top)
            total = jnp.sum(near, axis=1, keepdims=True)
            acc = dot(near.astype(BF16), qkv[2, here, :], NN)
            if first:
                total = total + jnp.sum(far, axis=1, keepdims=True)
                acc = acc + dot(far.astype(BF16), qkv[2, 0:first, :], NN)
            mixed.append(acc / total)
            flat = jnp.broadcast_to(top + jnp.log(total), (block, 128)).T
            lse[h : h + 1, here] = flat[0:1, :]
        both = jnp.where(lanes_of(0), mixed[0], mixed[1]).astype(BF16)
        for t in range(block // rows):
            out_s[order[i * (block // rows) + t]] = both[t * rows : (t + 1) * rows, :]
    for kr in range(2):
        for j in range(2 * tp):
            outs[j][kr] = out_s[kr * 2 * tp + j]


def cut(ref, i):
    width = ref.shape[-1]
    return slice(i * width, (i + 1) * width)


def pair_rows(pack, i, t_of, tp, e):
    own, mate = t_of[e], t_of[e ^ (tp // 2)]
    return jnp.concatenate(
        [pack[i, own, 0:64], pack[i, mate, 0:64], pack[i, own, 64:128], pack[i, mate, 64:128]],
        axis=0,
    )


def out_kernel(tp, t_of, seq_of, *refs):
    came, refs = refs[: 2 * tp], refs[2 * tp :]
    pack, own, send, acc = refs
    rows = own.shape[1]
    own[...] = jnp.zeros_like(own)
    acc[...] = jnp.zeros_like(acc)
    for e in range(tp):
        value = jnp.concatenate(
            [came[ys * tp + e][...].reshape(2 * rows, -1) for ys in range(2)], axis=1
        )
        s = seq_of[e]
        for i in range(pack.shape[0]):
            span = cut(pack, i)
            got = dot(value, pair_rows(pack, i, t_of, tp, e), NN)
            own[s, :, span] += got[:rows]
            acc[s, :, span] += got[rows:]
    send[...] = acc[...].astype(BF16)


def grad_mixed_kernel(tp, t_of, seq_of, own, got, pack, *outs):
    rows = own.shape[1]
    for e in range(tp):
        s, value = seq_of[e], 0.0
        for i in range(pack.shape[0]):
            span = cut(pack, i)
            left = jnp.concatenate([own[s, :, span], got[s, :, span]], axis=0)
            value = value + dot(left, pair_rows(pack, i, t_of, tp, e), NT)
        value = value.astype(BF16)
        for ys in range(2):
            for kr in range(2):
                outs[ys * tp + e][kr] = value[
                    kr * rows : (kr + 1) * rows, ys * 128 : (ys + 1) * 128
                ]


def chip_rows(own, got, span):
    seqs, rows = own.shape[0], own.shape[1]
    return jnp.concatenate(
        [own[:, :, span].reshape(seqs * rows, -1), got[:, :, span].reshape(seqs * rows, -1)],
        axis=0,
    )


def seq_rows(ref, e, s, seqs, rows):
    return jnp.concatenate(
        [ref[e, (j * seqs + s) * rows : (j * seqs + s + 1) * rows, :] for j in range(2)], axis=0
    )


def keys_values(kv_own, kv_far, e, s, keys):
    part = slice(s * keys, (s + 1) * keys)
    return (
        jnp.concatenate([kv_own[e, 0:64, part], kv_far[e, 0:64, part]], axis=0),
        jnp.concatenate([kv_own[e, 64:128, part], kv_far[e, 64:128, part]], axis=0),
    )


def pair_of(pack, i, t, j):
    return pack[i, t, j * 128 : (j + 1) * 128]


def all_pairs(pack, i, t_of, tp, j):
    return jnp.concatenate([pair_of(pack, i, t_of[e], j) for e in range(tp)], axis=0)


def by_pairs(own, got, pack, t_of, j, out):
    tp = out.shape[0]
    total = sum(
        dot(chip_rows(own, got, cut(pack, i)), all_pairs(pack, i, t_of, tp, j), NT)
        for i in range(pack.shape[0])
    ).astype(BF16)
    for e in range(tp):
        out[e] = total[:, e * 128 : (e + 1) * 128]


def pairs_back(value, pack, t_of, j, own, send):
    seqs, rows = own.shape[0], own.shape[1]
    half = seqs * rows
    left = jnp.concatenate([value[e] for e in range(value.shape[0])], axis=1)
    for i in range(pack.shape[0]):
        span = cut(pack, i)
        total = dot(left, all_pairs(pack, i, t_of, value.shape[0], j), NN)
        own[:, :, span] = total[:half].reshape(seqs, rows, -1)
        send[:, :, span] = total[half:].astype(BF16).reshape(seqs, rows, -1)


def keys_kernel(n_parts, tp, at, places, *refs):
    groups, refs = refs[:4], refs[4:]
    weights, (enc_all, kv) = refs[:n_parts], refs[n_parts:]
    seqs, keys = enc_all.shape[0], enc_all.shape[1]
    slots = keys // (4 * tp)
    rows = groups[0].shape[1] - seqs * slots
    for g in range(4):
        for e in range(tp):
            row = pl.ds(pl.multiple_of(places[g * tp + e] * slots, slots), slots)
            for s in range(seqs):
                enc_all[s, row, :] = groups[g][e, rows + s * slots : rows + (s + 1) * slots]
    for s in range(seqs):
        total = 0.0
        for i in range(n_parts):
            span = span_of(at, i, weights)
            total = total + dot(weights[i][-kv.shape[0] :], enc_all[s, :, span], NT)
        kv[:, s * keys : (s + 1) * keys] = total.astype(BF16)


def cross_kernel(tp, lengths, t_of, own_in, got_in, kv_own, kv_far, pack, own, send, q_out, o_out, lse):
    seqs, rows = own.shape[0], own.shape[1]
    keys = kv_own.shape[2] // seqs
    by_pairs(own_in, got_in, pack, t_of, 1, q_out)
    col = lax.broadcasted_iota(jnp.int32, (2 * rows, keys), 1)
    for s in range(seqs):
        valid = col < lengths[s]
        for e in range(tp):
            q = seq_rows(q_out, e, s, seqs, rows)
            keys_in, values_in = keys_values(kv_own, kv_far, e, s, keys)
            mixed = []
            for h in range(2):
                scores = jnp.where(valid, dot(head(q, h), keys_in, NN) * SCALE, MASKED)
                top = jnp.max(scores, axis=1, keepdims=True)
                probs = jnp.exp(scores - top)
                total = jnp.sum(probs, axis=1, keepdims=True)
                mixed.append(dot(probs.astype(BF16), values_in, NT) / total)
                flat = jnp.broadcast_to(top + jnp.log(total), (2 * rows, 128)).T
                row = (s * tp + e) * 2 + h
                lse[row : row + 1, :] = flat[0:1, :]
            both = jnp.where(lanes_of(0), mixed[0], mixed[1]).astype(BF16)
            for j in range(2):
                o_out[e, (j * seqs + s) * rows : (j * seqs + s + 1) * rows, :] = both[
                    j * rows : (j + 1) * rows
                ]
    pairs_back(o_out, pack, t_of, 2, own, send)


def cross_back_kernel(tp, lengths, t_of, own_in, got_in, q_in, lse, kv_own, kv_far, pack, *refs):
    own, send, dq_out, dkv_own, dkv_far, do_s = refs
    seqs, rows = own.shape[0], own.shape[1]
    keys = kv_own.shape[2] // seqs
    by_pairs(own_in, got_in, pack, t_of, 2, do_s)
    key = lax.broadcasted_iota(jnp.int32, (keys, 2 * rows), 0)
    for s in range(seqs):
        valid = key < lengths[s]
        for e in range(tp):
            q, g = seq_rows(q_in, e, s, seqs, rows), seq_rows(do_s, e, s, seqs, rows)
            keys_in, values_in = (v.T for v in keys_values(kv_own, kv_far, e, s, keys))
            dks, dvs, dq = [], [], 0.0
            for h in range(2):
                kh, vh = head(keys_in, h), head(values_in, h)
                row = (s * tp + e) * 2 + h
                scores = dot(kh, q, NT) * SCALE - lse[row : row + 1, :]
                probs = jnp.exp(jnp.where(valid, scores, MASKED))
                dp = dot(vh, g, NT)
                ds = (probs * (dp - jnp.sum(probs * dp, axis=0, keepdims=True))).astype(BF16)
                dvs.append(dot(probs.astype(BF16), g, NN)[:, h * 64 : (h + 1) * 64])
                dks.append(dot(ds, q, NN)[:, h * 64 : (h + 1) * 64] * SCALE)
                dq = dq + dot(ds, kh, TN)
            dq = (dq * SCALE).astype(BF16)
            for j in range(2):
                dq_out[e, (j * seqs + s) * rows : (j * seqs + s + 1) * rows, :] = dq[
                    j * rows : (j + 1) * rows
                ]
            part = slice(s * keys, (s + 1) * keys)
            dkv_own[e, :, part] = jnp.concatenate([dks[0], dvs[0]], axis=1).T.astype(BF16)
            dkv_far[e, :, part] = jnp.concatenate([dks[1], dvs[1]], axis=1).T.astype(BF16)
    pairs_back(dq_out, pack, t_of, 1, own, send)


def ffn_kernel(tp, n_own, n_got, y_own, y_got, weights, *refs):
    active, d_inner, d_own, d_send, o_own, o_send = refs
    seqs, rows = n_own.shape[0], n_own.shape[1]
    half, parts, width = seqs * rows, weights.shape[0], weights.shape[4]
    spans = [slice(i * width, (i + 1) * width) for i in range(parts)]
    n_rows = [chip_rows(n_own, n_got, span) for span in spans]
    y_rows = [chip_rows(y_own, y_got, span) for span in spans]
    for e in range(tp):
        inner = sum(
            dot(n_rows[i], weights[i, e, 0], NT) for i in range(parts)
        )
        grad = sum(
            dot(y_rows[i], weights[i, e, 1], NT) for i in range(parts)
        )
        square = inner * inner
        bend = jnp.tanh(0.7978845608 * (inner + 0.044715 * square * inner))
        active[e] = (0.5 * inner * (1.0 + bend)).astype(BF16)
        slope = 0.5 * (1.0 + bend) + 0.5 * inner * (1.0 - bend * bend) * (
            0.7978845608 * (1.0 + 3.0 * 0.044715 * square)
        )
        d_inner[e] = (grad * slope).astype(BF16)
    for j, (out, send, rows_in) in enumerate(((d_own, d_send, d_inner), (o_own, o_send, active))):
        left = jnp.concatenate([rows_in[e] for e in range(tp)], axis=1)
        for i in range(parts):
            total = dot(left, weights[i, :, j].reshape(left.shape[1], width), NN)
            out[:, :, spans[i]] = total[:half].reshape(seqs, rows, -1)
            send[:, :, spans[i]] = total[half:].astype(BF16).reshape(seqs, rows, -1)


def ffn_grad_kernel(tp, d_near, d_far, a_near, a_far, *refs):
    n_rows, y_rows, out = refs[:4], refs[4:8], refs[8]
    parts, width = out.shape[0], out.shape[4]
    for j, (near, far, given) in enumerate(
        ((d_near, d_far, n_rows), (a_near, a_far, y_rows))
    ):
        right = jnp.concatenate(
            [
                chip_rows(given[0], given[1], slice(None)),
                chip_rows(given[2], given[3], slice(None)),
            ],
            axis=0,
        )
        for e in range(tp):
            left = jnp.concatenate([near[e], far[e]], axis=0)
            value = dot(left, right, TN).astype(BF16)
            for i in range(parts):
                out[i, e, j] = value[:, i * width : (i + 1) * width]


def cross_grad_kernel(tp, dq, o, n_own, n_got, y_own, y_got, dkv_far, keep, send):
    parts, width = keep.shape[1], keep.shape[4]
    for j, (left, a, b) in enumerate(((dq, n_own, n_got), (o, y_own, y_got))):
        right = chip_rows(a, b, slice(None))
        for e in range(tp):
            got = dot(left[e], right, TN)
            for i in range(parts):
                span = slice(i * width, (i + 1) * width)
                keep[e, i, j] = got[0:64, span]
                send[e, (2 * i + j) * 64 : (2 * i + j + 1) * 64] = got[64:128, span].astype(BF16)
    send[:, 2 * parts * 64 :] = dkv_far[...]


def out_grad_kernel(tp, seq_of, own, got, *refs):
    came, (keep, send, acc) = refs[: 2 * tp], refs[2 * tp :]
    rows = own.shape[1]
    acc[...] = jnp.zeros_like(acc)
    for e in range(tp):
        s, mate = seq_of[e], e ^ (tp // 2)
        right = jnp.concatenate([own[s], got[s]], axis=0)
        for ys in range(2):
            left = came[ys * tp + e][...].reshape(2 * rows, -1)
            value = dot(left, right, TN)
            acc[ys, e] += value[0:64]
            acc[ys, mate] += value[64:128]
    keep[...] = acc[0]
    send[...] = acc[1].astype(BF16)


def enc_grad_kernel(n_parts, tp, at, places, d_kv, enc_all, *refs):
    weights, (keep, send, grad_w, all_s) = refs[:n_parts], refs[n_parts:]
    seqs, keys, model = enc_all.shape
    slots = keys // (4 * tp)
    total = 0.0
    for s in range(seqs):
        part = d_kv[:, s * keys : (s + 1) * keys]
        total = total + dot(part, enc_all[s], NN)
        for i in range(n_parts):
            all_s[s, :, span_of(at, i, weights)] = dot(part, weights[i][-d_kv.shape[0] :], TN)
    grad_w[...] = total
    for g in range(4):
        for e in range(tp):
            row = pl.ds(pl.multiple_of(places[g * tp + e] * slots, slots), slots)
            for s in range(seqs):
                if g < 2:
                    keep[g, e, s] = all_s[s, row, :]
                else:
                    send[g - 2, e, s] = all_s[s, row, :].astype(BF16)


def turn_kernel(count, offsets, *refs):
    pieces, outs = refs[:4], refs[4:-1]
    all_s = refs[-1]
    for j, out in enumerate(outs):
        part = pieces[0].shape[1]
        for i in range(4):
            all_s[pl.ds(pl.multiple_of(offsets[i] * part, part), part), :] = pieces[i][j].astype(F32)
        out[...] = all_s[...].T if j < count else all_s[...]


def qkv_grad_kernel(n_parts, tp, at, grads, *refs):
    groups, refs = refs[:4], refs[4:]
    weights, outs, sums = refs[:n_parts], refs[n_parts:-1], refs[-1]
    rows, columns = grads.shape[1], grads.shape[2]
    left = [grads[g * tp : (g + 1) * tp].reshape(-1, columns) for g in range(4)]
    ones = jnp.ones((8, left[0].shape[0]), BF16)
    counts = sum(dot(ones, part, NN) for part in left)
    turned = [part.T for part in left]
    for i in range(n_parts):
        span = span_of(at, i, outs)
        total = 0.0
        for g in range(4):
            right = groups[g][:, :rows, span].reshape(left[g].shape[0], -1)
            total = total + dot(turned[g], right, NN)
        outs[i][...] = total.astype(outs[i].dtype)
        weight = weights[i][0:columns].astype(F32)
        sums[0:1, span] = jnp.sum(total * weight, axis=0, keepdims=True)
        sums[1:2, span] = dot(counts, weight, NN, lax.Precision.HIGHEST)[0:1]


def self_back_kernel(n_parts, tp, block, at, order, qkv, lse, *refs):
    outs, grads, refs = refs[: 2 * tp], refs[2 * tp : 4 * tp], refs[4 * tp :]
    weights, (grad_qkv, keep, send, g_s, sum_s, dq_s) = refs[:n_parts], refs[n_parts:]
    length, width = qkv.shape[1], qkv.shape[2]
    rows = outs[0].shape[1]
    lane8 = lax.broadcasted_iota(jnp.int32, (8, width), 1)
    row8 = lax.broadcasted_iota(jnp.int32, (8, width), 0)
    chosen = jnp.where(lane8 // (width // 2) == row8, 1.0, 0.0).astype(F32)
    for j in range(2 * tp):
        for kr in range(2):
            r = kr * 2 * tp + j
            here = pl.ds(pl.multiple_of(order[r] * rows, rows), rows)
            g_s[here, :] = grads[j][kr]
            sum_s[:, here] = dot(
                chosen,
                grads[j][kr].astype(F32) * outs[j][kr].astype(F32),
                NT,
                lax.Precision.HIGHEST,
            )
    row = lax.broadcasted_iota(jnp.int32, (block, block), 0)
    col = lax.broadcasted_iota(jnp.int32, (block, block), 1)
    dq_s[...] = jnp.zeros_like(dq_s)
    blocks = length // block
    for j in range(blocks):
        here = slice(j * block, (j + 1) * block)
        kj, vj = qkv[1, here, :], qkv[2, here, :]
        dks, dvs = [], []
        for h in range(2):
            kh, vh = head(kj, h), head(vj, h)
            dk = dv = 0.0
            for i in range(j, blocks):
                there = slice(i * block, (i + 1) * block)
                q, g = qkv[0, there, :], g_s[there, :]
                scores = dot(kh, q, NT) * SCALE - lse[h : h + 1, there]
                if i == j:
                    scores = jnp.where(col >= row, scores, MASKED)
                probs = jnp.exp(scores)
                ds = (probs * (dot(vh, g, NT) - sum_s[h : h + 1, there])).astype(BF16)
                dv, dk = dv + dot(probs.astype(BF16), g, NN), dk + dot(ds, q, NN)
                dq_s[there, :] += dot(ds, kh, TN)
            dks.append(dk)
            dvs.append(dv)
        dk = (jnp.where(lanes_of(0), dks[0], dks[1]) * SCALE).astype(BF16)
        dv = jnp.where(lanes_of(0), dvs[0], dvs[1]).astype(BF16)
        qkv_rows = block // rows
        for t in range(qkv_rows):
            r, part = order[4 * tp + j * qkv_rows + t], slice(t * rows, (t + 1) * rows)
            grad_qkv[r, :, width : 2 * width] = dk[part]
            grad_qkv[r, :, 2 * width : 3 * width] = dv[part]
    for p in range(4 * tp):
        grad_qkv[order[4 * tp + p], :, 0:width] = (
            dq_s[p * rows : (p + 1) * rows, :] * SCALE
        ).astype(BF16)
    for g in (2, 3, 0, 1):
        left = grad_qkv[g * tp : (g + 1) * tp].reshape(tp * rows, -1)
        for i in range(n_parts):
            span = span_of(at, i, weights)
            value = dot(left, weights[i][0 : 3 * width], NN).reshape(tp, rows, -1)
            if g < 2:
                keep[g, :, :, span] = value
            else:
                send[g - 2, :, :, span] = value.astype(BF16)


def swap(value, axis, bit):
    return lax.ppermute(value, axis, [(i, i ^ bit) for i in range(lax.axis_size(axis))])


def swap_core(value):
    return swap(value, "ctx", 1)


def swap_y(value):
    return swap(value, "ctx", 2)


def from_tp(value, step):
    return swap(value, "tp", step)


def from_chip(value, far, step):
    ctx, size = lax.axis_size("ctx"), lax.axis_size("tp")
    if far == 0 and step == 0:
        return value
    pairs = [
        ((c ^ (2 * far)) * size + (i ^ step), c * size + i)
        for c in range(ctx)
        for i in range(size)
    ]
    return lax.ppermute(value, ("ctx", "tp"), pairs)


def after(value, *others):
    return lax.optimization_barrier((value, others))[0]


def pick(value, index, axis):
    return lax.dynamic_index_in_dim(value, index, axis, keepdims=False)


def gather_tp(value):
    return jnp.stack([value] + [from_tp(value, e) for e in range(1, lax.axis_size("tp"))])


def model_parts(value):
    if lax.axis_size("fsdp") == 2:
        return (value, swap(value, "fsdp", 1))
    return (lax.all_gather(value, "fsdp", axis=value.ndim - 1, tiled=True),)


def sum_model(value):
    if lax.axis_size("fsdp") != 2:
        return lax.psum_scatter(
            value.astype(BF16), "fsdp", scatter_dimension=value.ndim - 1, tiled=True
        ).astype(F32)
    width, mine = value.shape[-1] // 2, lax.axis_index("fsdp")
    keep = lax.dynamic_slice_in_dim(value, mine * width, width, value.ndim - 1)
    send = lax.dynamic_slice_in_dim(value, (1 - mine) * width, width, value.ndim - 1)
    return keep.astype(F32) + swap(send.astype(BF16), "fsdp", 1).astype(F32)


def sum_parts(parts):
    if len(parts) == 1:
        return sum_model(parts[0])
    return parts[0].astype(F32) + swap(parts[1], "fsdp", 1).astype(F32)


def sum_tp(pieces):
    total = pieces[0].astype(F32)
    for e in range(1, lax.axis_size("tp")):
        total = total + from_tp(pieces[e].astype(BF16), e).astype(F32)
    return total


def sum_all(value):
    for axis in ("ctx", "tp", "fsdp"):
        if axis == "fsdp" and lax.axis_size(axis) != 2:
            value = lax.psum(value, axis)
            continue
        bit = 1
        while bit < lax.axis_size(axis):
            value = value + swap(value, axis, bit)
            bit *= 2
    return value


def shards(
    tokens,
    enc_states,
    enc_lengths,
    cotangent,
    gain_self,
    shift_self,
    w_query,
    w_key,
    w_value,
    w_out,
    gain_cross,
    shift_cross,
    cross_query,
    cross_key,
    cross_value,
    cross_out,
    gain_ffn,
    shift_ffn,
    w_inner,
    w_outer,
):
    seqs, rows, model = tokens.shape
    tp, ctx = lax.axis_size("tp"), lax.axis_size("ctx")
    z, c = lax.axis_index("tp"), lax.axis_index("ctx")
    y, k = c // 2, c % 2
    span = tp // 2
    local = w_query.shape[0]
    hid = w_inner.shape[1] // ctx
    own_rows = tokens.shape
    chip = 2 * seqs * rows
    n_parts = 2 if lax.axis_size("fsdp") == 2 else 1
    mine = lax.axis_index("fsdp") * local if n_parts == 2 else 0
    at = jnp.stack([jnp.int32(mine), jnp.int32(model // 2 - mine)])
    step = jnp.arange(tp, dtype=jnp.int32)
    seq_of = (z ^ step) // span
    two = lambda vector: vector.reshape(1, -1)
    gains = [two(g) for g in (gain_self, shift_self, gain_cross, shift_cross, gain_ffn, shift_ffn)]

    rel = jnp.arange(4 * tp, dtype=jnp.int32)
    places = (2 * ((rel // tp) % 2 ^ y) + ((rel // (2 * tp)) ^ k)) * tp + ((rel % tp) ^ z)
    order = ((((rel // tp) % 2) ^ k) * 2 + ((rel // (2 * tp)) ^ y)) * tp + ((rel % tp) ^ z)
    places, order = places.astype(jnp.int32), order.astype(jnp.int32)

    def own_head(weight):
        return lax.dynamic_slice_in_dim(weight, c * HEAD_DIM, HEAD_DIM, 0)

    def core_half(weight):
        other = lax.dynamic_slice_in_dim(weight, (c ^ 2) * HEAD_DIM, HEAD_DIM, 0)
        return jnp.concatenate([own_head(weight), other])

    own_qkv = jnp.stack([own_head(w.T) for w in (w_query, w_key, w_value)])
    own_ckv = jnp.concatenate([own_head(cross_key.T), own_head(cross_value.T)])
    own_qkv, picks = lax.optimization_barrier((own_qkv, (z ^ step) // span))
    other_qkv = from_tp(own_qkv, span)
    slots = enc_states.shape[1]
    keys = 4 * tp * slots
    pieces = kernel_call(
        functools.partial(first_norm_kernel, tp),
        "norm_self",
        [picks],
        [tokens, enc_states, gains[0], gains[1]],
        [shape((rows + seqs * slots, model), BF16)] * tp,
        [pltpu.VMEM(own_rows, BF16)],
    )
    t_of = (z ^ step).astype(jnp.int32)
    pack = jnp.concatenate([core_half(w) for w in (w_out, cross_query.T, cross_out)])

    def gather_weights(value):
        got = lax.all_gather(value, ("fsdp", "tp"))
        got = got.reshape(-1, tp, *value.shape)
        if n_parts == 2:
            return got
        return jnp.moveaxis(got, 0, -2).reshape(1, tp, *value.shape[:-1], model)

    which = jnp.stack([c, c ^ 1, c ^ 2, c ^ 3]).astype(jnp.int32)
    near = [pieces[0]] + [None] * (tp - 1)
    bit = span
    while bit:
        for e in range(0, tp, 2 * bit):
            near[e + bit] = from_tp(pieces[bit] if e == 0 else near[e], bit)
        bit //= 2
    far = [swap_y(piece) for piece in near]
    near = jnp.stack(after(near, other_qkv, far[0]))
    h_qkv = model_parts(
        jnp.concatenate([jnp.stack([own_qkv, other_qkv], 1).reshape(-1, local), own_ckv])
    )
    far = after(jnp.stack(far), h_qkv)
    groups = [near, far, swap_core(near), swap_core(far)]

    h_ffn = jnp.stack(
        [
            lax.dynamic_slice_in_dim(w_inner, c * hid, hid, 1).T,
            lax.dynamic_slice_in_dim(w_outer, c * hid, hid, 0),
        ]
    )
    pack = gather_weights(after(pack, near))
    h_ffn = gather_weights(after(h_ffn, near))
    y_far = swap_y(after(cotangent, far))
    y_rows = [cotangent, swap_core(after(cotangent, near)), y_far]

    enc_all, kv_own = kernel_call(
        functools.partial(keys_kernel, n_parts, tp),
        "cross_keys",
        [at, places],
        [*groups, *h_qkv],
        [shape((seqs, keys, model), BF16), shape((2 * HEAD_DIM, seqs * keys), BF16)],
        flops=4 * seqs * keys * model * 2 * HEAD_DIM,
    )
    kv_at = kv_own
    kv_own = gather_tp(kv_own)

    length, width = ctx * tp * rows, 2 * HEAD_DIM
    qkv, lse_self, *o_sent = kernel_call(
        functools.partial(self_kernel, n_parts, tp, BLOCK),
        "self_attend",
        [after(at, kv_at), places, order],
        [*groups, *h_qkv],
        [shape((3, length, width), BF16), shape((2, length), F32)]
        + [shape((2, rows, width), BF16)] * (2 * tp),
        [pltpu.VMEM((4 * tp, rows, width), BF16)],
        flops=4 * length * length * width + 6 * length * model * width,
    )
    o_sent = after(o_sent, kv_own)
    kv_far = swap_y(kv_own)
    came = [
        from_chip(o_sent[ys * tp + e], ys, e) for ys in range(2) for e in range(tp)
    ]
    partial_own, partial_send = kernel_call(
        functools.partial(out_kernel, tp),
        "out_self",
        [t_of, seq_of],
        [*came, pack],
        [shape(own_rows, F32), shape(own_rows, BF16)],
        [pltpu.VMEM(own_rows, F32)],
        flops=2 * chip * 4 * width * model,
    )

    def add_norm(before, own, sent, which):
        return kernel_call(
            norm_kernel,
            "add_norm",
            [],
            [before, own, swap_core(sent), gains[2 * which], gains[2 * which + 1]],
            [shape(own_rows, F32), shape(own_rows, BF16)],
        )

    hidden1, n2 = add_norm(tokens, partial_own, partial_send, 1)

    n2_got = swap_core(n2)
    partial_own, partial_send, q_cross, o_cross, lse_cross = kernel_call(
        functools.partial(cross_kernel, tp),
        "cross_attend",
        [enc_lengths, after(t_of, y_far)],
        [n2, n2_got, kv_own, kv_far, pack],
        [
            shape(own_rows, F32),
            shape(own_rows, BF16),
            shape((tp, chip, width), BF16),
            shape((tp, chip, width), BF16),
            shape((seqs * tp * 2, 2 * rows), F32),
        ],
        flops=4 * chip * tp * width * (model + keys),
    )
    hidden2, n3 = add_norm(hidden1, partial_own, partial_send, 2)

    n3_far = swap_y(n3)
    y_rows.append(swap_core(after(y_far, n3)))
    n_rows = [n3, swap_core(n3), n3_far, swap_core(n3_far)]

    def feed(first):
        return kernel_call(
            functools.partial(ffn_kernel, tp),
            "feed_forward",
            [],
            [*n_rows[first : first + 2], *y_rows[first : first + 2], h_ffn],
            [shape((tp, chip, hid), BF16)] * 2 + [shape(own_rows, F32), shape(own_rows, BF16)] * 2,
            flops=8 * chip * model * tp * hid,
        )

    a_far, d_far, dn_far, dn_far_send, out_far, out_far_send = feed(2)
    a_near, d_near, dn_own, dn_near_send, out_own, out_near_send = feed(0)

    def far_sum(own, sent):
        return (own + swap_core(sent).astype(F32)).astype(BF16)

    dn_near = swap_core(dn_near_send)
    dn_far = far_sum(dn_far, dn_far_send)
    g_ffn = kernel_call(
        functools.partial(ffn_grad_kernel, tp),
        "grad_feed_forward",
        [],
        [after(d_near, dn_far, dn_near), d_far, a_near, a_far, *n_rows, *y_rows],
        [shape((n_parts, tp, 2, hid, model // n_parts), BF16)],
        flops=8 * chip * model * tp * hid,
    )[0]
    dn_far = swap_y(dn_far)

    def norm_back(hidden, gain, before, own, *got):
        return kernel_call(
            norm_back_kernel,
            "norm_back",
            [],
            [hidden, gain, before, own, *got],
            [shape(own_rows, F32), shape(own_rows, BF16), shape((2, model), F32)],
        )

    grad2, y2, sums_ffn = norm_back(
        hidden2, after(gains[4], g_ffn), cotangent, dn_own, dn_near, dn_far
    )
    if n_parts == 1:
        g_ffn = g_ffn.reshape(tp, 2, hid, -1, local).transpose(3, 0, 1, 2, 4)
    g_ffn = lax.psum_scatter(
        after(g_ffn.reshape(-1, 2, hid, local), y2), ("fsdp", "tp"), scatter_dimension=0
    )
    g_ffn = lax.all_gather(g_ffn.astype(BF16), "ctx", axis=1, tiled=True)

    y2_got = swap_core(y2)
    held, out_near_send, out_far_send = after((out_far, out_near_send, out_far_send), y2)
    out_near, out_far = swap_core(out_near_send), far_sum(held, out_far_send)
    dn_own, dn_send, dq_cross, dkv_own, dkv_far = kernel_call(
        functools.partial(cross_back_kernel, tp),
        "cross_attend_back",
        [enc_lengths, after(t_of, out_near, out_far)],
        [y2, y2_got, q_cross, lse_cross, kv_own, kv_far, pack],
        [
            shape(own_rows, F32),
            shape(own_rows, BF16),
            shape((tp, chip, width), BF16),
            shape(kv_own.shape, BF16),
            shape(kv_own.shape, BF16),
        ],
        [pltpu.VMEM((tp, chip, width), BF16)],
        flops=4 * chip * tp * width * (model + 3 * keys),
    )
    out_far = swap_y(out_far)
    dn_send = after(dn_send, out_far)
    dn_got = swap_core(dn_send)
    half = seqs * keys
    halves = model // half
    keep, send = kernel_call(
        functools.partial(cross_grad_kernel, tp),
        "grad_cross",
        [],
        [dq_cross, o_cross, n2, n2_got, y2, y2_got, dkv_far],
        [
            shape((tp, halves, 2, HEAD_DIM, half), F32),
            shape((tp, 2 * halves * HEAD_DIM + width, half), BF16),
        ],
        flops=4 * chip * tp * width * model,
    )
    cross_got = swap_y(send)
    grad1, y1, sums_cross = norm_back(hidden1, gains[2], grad2, dn_own, dn_got)

    y1_got = swap_core(y1)
    do_sent = kernel_call(
        functools.partial(grad_mixed_kernel, tp),
        "grad_mixed",
        [t_of, seq_of],
        [y1, y1_got, pack],
        [shape((2, rows, width), BF16)] * (2 * tp),
        flops=2 * chip * 4 * width * model,
    )
    do_came = [
        from_chip(do_sent[ys * tp + e], ys, e) for ys in range(2) for e in range(tp)
    ]
    out_keep, out_send = kernel_call(
        functools.partial(out_grad_kernel, tp),
        "grad_out",
        [after(seq_of, do_sent)],
        [y1, y1_got, *came],
        [shape((tp, HEAD_DIM, model), F32), shape((tp, HEAD_DIM, model), BF16)],
        [pltpu.VMEM((2, tp, HEAD_DIM, model), F32)],
        flops=2 * chip * tp * width * model,
    )
    cross_got = after(cross_got, do_came)
    g_cross = keep + cross_got[:, :-width].reshape(keep.shape).astype(F32)
    d_kv = dkv_own.astype(F32) + cross_got[:, -width:].astype(F32)
    first = lax.axis_index("fsdp") if n_parts == 2 else 0
    cross_x = swap(pick(g_cross, 1 - first, 1).astype(BF16), "fsdp", 1) if n_parts == 2 else None
    out_got = swap_y(after(out_send, do_came))
    d_qkv, dn_keep, dn_send = kernel_call(
        functools.partial(self_back_kernel, n_parts, tp, BLOCK),
        "self_attend_back",
        [after(at, out_keep, g_cross), jnp.concatenate([places, order])],
        [qkv, lse_self, *o_sent, *do_came, *h_qkv],
        [
            shape((4 * tp, rows, 3 * width), BF16),
            shape((2, tp, rows, model), F32),
            shape((2, tp, rows, model), BF16),
        ],
        [
            pltpu.VMEM((length, width), BF16),
            pltpu.VMEM((8, length), F32),
            pltpu.VMEM((length, width), F32),
        ],
        flops=10 * length * length * width + 6 * length * model * width,
    )
    dn_send, dn_keep, cross_x, out_got, out_far = after(
        (dn_send, dn_keep, cross_x, out_got, out_far), d_qkv
    )
    dn_got = swap_core(dn_send)
    dn_sent = [(dn_keep[1, e] + dn_got[1, e].astype(F32)).astype(BF16) for e in range(tp)]
    dn_near = [dn_keep[0, e] + dn_got[0, e].astype(F32) for e in range(tp)]
    g_cross, d_kv, cross_x, out_got, out_far = after(
        (g_cross, d_kv, cross_x, out_got, out_far), dn_sent
    )
    dn_upper = swap_y(jnp.stack(dn_sent[span:]))
    dn_lower = swap_y(jnp.stack(dn_sent[:span]))
    if n_parts == 2:
        g_cross = pick(g_cross, first, 1) + cross_x.astype(F32)
        g_cross = sum_tp(jnp.concatenate([g_cross.reshape(tp, -1, local), d_kv], axis=1))
        g_cross = after(g_cross, dn_upper)
        g_cross, d_kv = g_cross[: 2 * HEAD_DIM].reshape(2, HEAD_DIM, local), g_cross[2 * HEAD_DIM :]
    else:
        g_cross = sum_tp(
            sum_model(g_cross.transpose(0, 2, 3, 1, 4).reshape(tp, 2, HEAD_DIM, model))
        )
        d_kv = sum_tp(d_kv)
    out_tokens = (hidden2 + out_own + out_near.astype(F32) + out_far.astype(F32)).astype(BF16)
    grad_inner, grad_outer = after(g_ffn[0], dn_sent).T.astype(F32), g_ffn[1].astype(F32)
    *g_qkv, sums_self = kernel_call(
        functools.partial(qkv_grad_kernel, n_parts, tp),
        "grad_qkv",
        [after(at, dn_upper, grad_inner, grad_outer)],
        [d_qkv, *groups, *h_qkv],
        (
            [shape((3 * width, model), F32)]
            if n_parts == 1
            else [shape((3 * width, local), F32), shape((3 * width, local), BF16)]
        )
        + [shape((2, model), F32)],
        flops=6 * length * width * model,
    )
    enc_keep, enc_send, g_ckv = kernel_call(
        functools.partial(enc_grad_kernel, n_parts, tp),
        "grad_enc",
        [at, places],
        [d_kv.astype(BF16), enc_all, *h_qkv],
        [
            shape((2, tp, seqs, slots, model), F32),
            shape((2, tp, seqs, slots, model), BF16),
            shape((2 * HEAD_DIM, model), F32),
        ],
        [pltpu.VMEM((seqs, keys, model), F32)],
        flops=4 * seqs * keys * width * model,
    )
    enc_got = swap_core(enc_send)
    enc_far = swap_y((enc_keep[1] + enc_got[1].astype(F32)).astype(BF16))
    grad_enc = sum_tp(enc_keep[0] + enc_got[0].astype(F32) + enc_far.astype(F32))
    g_out = sum_model(out_keep + out_got.astype(F32))
    dn_pieces = [dn_near[e] + dn_lower[e].astype(F32) for e in range(span)]
    dn_pieces += [dn_near[span + e] + dn_upper[e].astype(F32) for e in range(span)]
    for first_piece in (span, 0):
        count = span
        while count > 1:
            count //= 2
            for e in range(count):
                got = from_tp(dn_pieces[first_piece + count + e].astype(BF16), count)
                if first_piece:
                    dn_began = got
                dn_pieces[first_piece + e] = dn_pieces[first_piece + e] + got.astype(F32)
    dn_other = from_tp(dn_pieces[span].astype(BF16), span)
    grad_tokens = kernel_call(
        last_norm_kernel,
        "norm_back_self",
        [seq_of],
        [tokens, gains[0], grad1, dn_pieces[0], dn_other],
        [shape(own_rows, F32)],
        [pltpu.VMEM(own_rows, F32)],
    )[0]

    sums = jnp.concatenate([sums_self, sums_cross, sums_ffn])
    sums = sum_all(after(sums, dn_other))
    grad_shift_self = sums[1]
    grad_gain_self = (sums[0] - shift_self * sums[1]) / gain_self

    def turned(pieces, count):
        quarters = pieces[0].shape[0]
        return kernel_call(
            functools.partial(turn_kernel, count),
            "turn",
            [which],
            pieces,
            [
                shape((pieces[0].shape[2], 4 * pieces[0].shape[1])[:: 1 if j < count else -1], F32)
                for j in range(quarters)
            ],
            [pltpu.VMEM((4 * pieces[0].shape[1], pieces[0].shape[2]), F32)],
        )

    def along_ctx(value):
        far = swap_y(value)
        return [value, swap_core(value), far, swap_core(far)]


    g_cross = jnp.concatenate([sum_model(g_ckv).reshape(2, HEAD_DIM, local), g_cross]).astype(BF16)
    g_cross = lax.all_gather(g_cross, "ctx", axis=1, tiled=True).astype(F32)
    g_qkv, g_out = after((sum_parts(g_qkv), g_out), dn_began)
    g_qkv = g_qkv.reshape(3, 2, HEAD_DIM, local)
    total, g_mate = g_out[0], g_qkv[:, 1].reshape(-1, local)
    for e in range(1, tp):
        piece = g_out[e]
        if e == span:
            got = from_tp(jnp.concatenate([piece, g_mate]).astype(BF16), e).astype(F32)
            total, g_mate = total + got[:HEAD_DIM], got[HEAD_DIM:]
        else:
            total = total + from_tp(piece.astype(BF16), e).astype(F32)
    g_qkv = g_qkv[:, 0] + g_mate.reshape(3, HEAD_DIM, local)
    g_self = jnp.concatenate([g_qkv, total[None]]).astype(BF16)
    g_self = turned(along_ctx(g_self), 3)
    return (
        out_tokens,
        grad_tokens,
        grad_enc,
        grad_gain_self,
        grad_shift_self,
        g_self[0],
        g_self[1],
        g_self[2],
        g_self[3],
        sums[2],
        sums[3],
        g_cross[2].T,
        g_cross[0].T,
        g_cross[1].T,
        g_cross[3],
        sums[4],
        sums[5],
        grad_inner,
        grad_outer,
    )


def solution(mesh):
    in_specs = (
        P("fsdp", ("ctx", "tp"), None),
        P("fsdp", ("ctx", "tp"), None),
        P("fsdp"),
        P("fsdp", ("ctx", "tp"), None),
        P(),
        P(),
        P("fsdp", "tp"),
        P("fsdp", "tp"),
        P("fsdp", "tp"),
        P("tp", "fsdp"),
        P(),
        P(),
        P("fsdp", "tp"),
        P("fsdp", "tp"),
        P("fsdp", "tp"),
        P("tp", "fsdp"),
        P(),
        P(),
        P("fsdp", "tp"),
        P("tp", "fsdp"),
    )
    out_specs = (
        P("fsdp", ("ctx", "tp"), None),
        P("fsdp", ("ctx", "tp"), None),
        P("fsdp", ("ctx", "tp"), None),
        P(),
        P(),
        P("fsdp", "tp"),
        P("fsdp", "tp"),
        P("fsdp", "tp"),
        P("tp", "fsdp"),
        P(),
        P(),
        P("fsdp", "tp"),
        P("fsdp", "tp"),
        P("fsdp", "tp"),
        P("tp", "fsdp"),
        P(),
        P(),
        P("fsdp", "tp"),
        P("tp", "fsdp"),
    )
    return jax.shard_map(shards, mesh=mesh, in_specs=in_specs, out_specs=out_specs, check_vma=False)
```

```python
import functools

import jax
import jax.numpy as jnp
from jax import lax
from jax.experimental import pallas as pl
from jax.experimental.pallas import tpu as pltpu
from jax.sharding import PartitionSpec as P

HEAD_DIM = 64
SCALE = HEAD_DIM ** (-0.5)
BLOCK = 512
MASKED = -1e30
EPS = 1e-05
F32 = jnp.float32
BF16 = jnp.bfloat16
NT = (((1,), (1,)), ((), ()))
NN = (((1,), (0,)), ((), ()))
TN = (((0,), (0,)), ((), ()))


def dot(left, right, dims, precision=None):
    return lax.dot_general(left, right, dims, preferred_element_type=F32, precision=precision)


def shape(dims, dtype):
    return jax.ShapeDtypeStruct(tuple(dims), dtype)


def kernel_call(body, name, scalars, arrays, outs, scratch=(), flops=0):
    vmem = pl.BlockSpec(memory_space=pltpu.VMEM)
    smem = pl.BlockSpec(memory_space=pltpu.SMEM)
    moved = sum(a.size * a.dtype.itemsize for a in arrays)
    moved += sum(a.size * a.dtype.itemsize for a in outs)
    return pl.pallas_call(
        body,
        out_shape=tuple(outs),
        in_specs=[smem] * len(scalars) + [vmem] * len(arrays),
        out_specs=(vmem,) * len(outs),
        scratch_shapes=list(scratch),
        compiler_params=pltpu.CompilerParams(vmem_limit_bytes=56 << 20),
        cost_estimate=pl.CostEstimate(flops=flops // 1, bytes_accessed=moved // 1, transcendentals=0),
        name=name,
    )(*scalars, *arrays)


def span_of(at, i, parts):
    width = parts[i].shape[-1]
    return pl.ds(pl.multiple_of(at[i], 128), width) if len(parts) > 1 else slice(0, width)


def onto(read, parts, at, rows_of=lambda part: part[...]):
    return sum(
        dot(read(span_of(at, i, parts)), rows_of(part), NT) for i, part in enumerate(parts)
    )


def lanes_of(h, width=128):
    return (lax.broadcasted_iota(jnp.int32, (1, width), 1) < width // 2) == (h == 0)


def head(value, h):
    return jnp.where(lanes_of(h), value, jnp.zeros_like(value))


def normal(hidden, gain, shift):
    centre = hidden - jnp.mean(hidden, axis=-1, keepdims=True)
    spread = jnp.mean(centre * centre, axis=-1, keepdims=True)
    return centre * lax.rsqrt(spread + EPS) * gain + shift


def first_norm_kernel(tp, picks, tokens, enc, gain, shift, *rest):
    outs, keep = rest[:tp], rest[tp]
    rows, slots = tokens.shape[1], enc.shape[1]
    for s in range(tokens.shape[0]):
        keep[s] = normal(tokens[s].astype(F32), gain[...], shift[...]).astype(BF16)
    for e in range(tp):
        outs[e][:rows] = keep[picks[e]]
        for s in range(enc.shape[0]):
            outs[e][rows + s * slots : rows + (s + 1) * slots] = enc[s]


def norm_kernel(before, own, got, gain, shift, hidden, normed):
    for s in range(before.shape[0]):
        value = before[s].astype(F32) + own[s] + got[s].astype(F32)
        hidden[s] = value
        normed[s] = normal(value, gain[...], shift[...]).astype(BF16)


def norm_back_rows(hidden, gain, grad):
    centre = hidden - jnp.mean(hidden, axis=-1, keepdims=True)
    rate = lax.rsqrt(jnp.mean(centre * centre, axis=-1, keepdims=True) + EPS)
    unit, scaled = centre * rate, grad * gain
    back = rate * (
        scaled
        - jnp.mean(scaled, axis=-1, keepdims=True)
        - unit * jnp.mean(scaled * unit, axis=-1, keepdims=True)
    )
    return back, jnp.sum(grad * unit, axis=0, keepdims=True), jnp.sum(grad, axis=0, keepdims=True)


def norm_back_kernel(hidden, gain, after, own, *rest):
    got, (grad_out, rounded, sums) = rest[:-3], rest[-3:]
    gains = shifts = None
    for s in range(hidden.shape[0]):
        grad = own[s]
        for more in got:
            grad = grad + more[s].astype(F32)
        back, g, b = norm_back_rows(hidden[s], gain[...], grad)
        gains, shifts = (g, b) if gains is None else (gains + g, shifts + b)
        total = after[s].astype(F32) + back
        grad_out[s] = total
        rounded[s] = total.astype(BF16)
    sums[0:1, :] = gains
    sums[1:2, :] = shifts


def last_norm_kernel(seq_of, tokens, gain, after, own, other, grad_out, acc):
    acc[seq_of[0]] = own[...]
    acc[1 - seq_of[0]] = other[...].astype(F32)
    for s in range(tokens.shape[0]):
        back, _, _ = norm_back_rows(tokens[s].astype(F32), gain[...], acc[s])
        grad_out[s] = after[s] + back


def self_kernel(n_parts, tp, block, at, places, order, *refs):
    groups, refs = refs[:4], refs[4:]
    weights, refs = refs[:n_parts], refs[n_parts:]
    qkv, lse, outs, out_s = refs[0], refs[1], refs[2:-1], refs[-1]
    rows, width = out_s.shape[1], qkv.shape[2]
    length = qkv.shape[1]
    for g in range(4):
        group = groups[g]
        value = onto(
            lambda span: group[:, :rows, span].reshape(tp * rows, -1),
            weights,
            at,
            lambda part: part[0 : 3 * width],
        ).astype(BF16)
        for e in range(tp):
            row = pl.ds(pl.multiple_of(places[g * tp + e] * rows, rows), rows)
            for i in range(3):
                qkv[i, row, :] = value[e * rows : (e + 1) * rows, i * width : (i + 1) * width]
    row = lax.broadcasted_iota(jnp.int32, (block, block), 0)
    col = lax.broadcasted_iota(jnp.int32, (block, block), 1)
    for i in range(length // block):
        first, here = i * block, slice(i * block, (i + 1) * block)
        q = qkv[0, here, :]
        mixed = []
        for h in range(2):
            qh = head(q, h)
            near = jnp.where(row >= col, dot(qh, qkv[1, here, :], NT) * SCALE, MASKED)
            top = jnp.max(near, axis=1, keepdims=True)
            if first:
                far = dot(qh, qkv[1, 0:first, :], NT) * SCALE
                top = jnp.maximum(top, jnp.max(far, axis=1, keepdims=True))
                far = jnp.exp(far - top)
            near = jnp.exp(near - top)
            total = jnp.sum(near, axis=1, keepdims=True)
            acc = dot(near.astype(BF16), qkv[2, here, :], NN)
            if first:
                total = total + jnp.sum(far, axis=1, keepdims=True)
                acc = acc + dot(far.astype(BF16), qkv[2, 0:first, :], NN)
            mixed.append(acc / total)
            flat = jnp.broadcast_to(top + jnp.log(total), (block, 128)).T
            lse[h : h + 1, here] = flat[0:1, :]
        both = jnp.where(lanes_of(0), mixed[0], mixed[1]).astype(BF16)
        for t in range(block // rows):
            out_s[order[i * (block // rows) + t]] = both[t * rows : (t + 1) * rows, :]
    for kr in range(2):
        for j in range(2 * tp):
            outs[j][kr] = out_s[kr * 2 * tp + j]


def cut(ref, i):
    width = ref.shape[-1]
    return slice(i * width, (i + 1) * width)


def pair_rows(pack, i, t_of, tp, e):
    own, mate = t_of[e], t_of[e ^ (tp // 2)]
    return jnp.concatenate(
        [pack[i, own, 0:64], pack[i, mate, 0:64], pack[i, own, 64:128], pack[i, mate, 64:128]],
        axis=0,
    )


def out_kernel(tp, t_of, seq_of, *refs):
    came, refs = refs[: 2 * tp], refs[2 * tp :]
    pack, own, send, acc = refs
    rows = own.shape[1]
    own[...] = jnp.zeros_like(own)
    acc[...] = jnp.zeros_like(acc)
    for e in range(tp):
        value = jnp.concatenate(
            [came[ys * tp + e][...].reshape(2 * rows, -1) for ys in range(2)], axis=1
        )
        s = seq_of[e]
        for i in range(pack.shape[0]):
            span = cut(pack, i)
            got = dot(value, pair_rows(pack, i, t_of, tp, e), NN)
            own[s, :, span] += got[:rows]
            acc[s, :, span] += got[rows:]
    send[...] = acc[...].astype(BF16)


def grad_mixed_kernel(tp, t_of, seq_of, own, got, pack, *outs):
    rows = own.shape[1]
    for e in range(tp):
        s, value = seq_of[e], 0.0
        for i in range(pack.shape[0]):
            span = cut(pack, i)
            left = jnp.concatenate([own[s, :, span], got[s, :, span]], axis=0)
            value = value + dot(left, pair_rows(pack, i, t_of, tp, e), NT)
        value = value.astype(BF16)
        for ys in range(2):
            for kr in range(2):
                outs[ys * tp + e][kr] = value[
                    kr * rows : (kr + 1) * rows, ys * 128 : (ys + 1) * 128
                ]


def chip_rows(own, got, span):
    seqs, rows = own.shape[0], own.shape[1]
    return jnp.concatenate(
        [own[:, :, span].reshape(seqs * rows, -1), got[:, :, span].reshape(seqs * rows, -1)],
        axis=0,
    )


def seq_rows(ref, e, s, seqs, rows):
    return jnp.concatenate(
        [ref[e, (j * seqs + s) * rows : (j * seqs + s + 1) * rows, :] for j in range(2)], axis=0
    )


def keys_values(kv_own, kv_far, e, s, keys):
    part = slice(s * keys, (s + 1) * keys)
    return (
        jnp.concatenate([kv_own[e, 0:64, part], kv_far[e, 0:64, part]], axis=0),
        jnp.concatenate([kv_own[e, 64:128, part], kv_far[e, 64:128, part]], axis=0),
    )


def pair_of(pack, i, t, j):
    return pack[i, t, j * 128 : (j + 1) * 128]


def all_pairs(pack, i, t_of, tp, j):
    return jnp.concatenate([pair_of(pack, i, t_of[e], j) for e in range(tp)], axis=0)


def by_pairs(own, got, pack, t_of, j, out):
    tp = out.shape[0]
    total = sum(
        dot(chip_rows(own, got, cut(pack, i)), all_pairs(pack, i, t_of, tp, j), NT)
        for i in range(pack.shape[0])
    ).astype(BF16)
    for e in range(tp):
        out[e] = total[:, e * 128 : (e + 1) * 128]


def pairs_back(value, pack, t_of, j, own, send):
    seqs, rows = own.shape[0], own.shape[1]
    half = seqs * rows
    left = jnp.concatenate([value[e] for e in range(value.shape[0])], axis=1)
    for i in range(pack.shape[0]):
        span = cut(pack, i)
        total = dot(left, all_pairs(pack, i, t_of, value.shape[0], j), NN)
        own[:, :, span] = total[:half].reshape(seqs, rows, -1)
        send[:, :, span] = total[half:].astype(BF16).reshape(seqs, rows, -1)


def keys_kernel(n_parts, tp, at, places, *refs):
    groups, refs = refs[:4], refs[4:]
    weights, (enc_all, kv) = refs[:n_parts], refs[n_parts:]
    seqs, keys = enc_all.shape[0], enc_all.shape[1]
    slots = keys // (4 * tp)
    rows = groups[0].shape[1] - seqs * slots
    for g in range(4):
        for e in range(tp):
            row = pl.ds(pl.multiple_of(places[g * tp + e] * slots, slots), slots)
            for s in range(seqs):
                enc_all[s, row, :] = groups[g][e, rows + s * slots : rows + (s + 1) * slots]
    for s in range(seqs):
        total = 0.0
        for i in range(n_parts):
            span = span_of(at, i, weights)
            total = total + dot(weights[i][-kv.shape[0] :], enc_all[s, :, span], NT)
        kv[:, s * keys : (s + 1) * keys] = total.astype(BF16)


def cross_kernel(tp, lengths, t_of, own_in, got_in, kv_own, kv_far, pack, own, send, q_out, o_out, lse):
    seqs, rows = own.shape[0], own.shape[1]
    keys = kv_own.shape[2] // seqs
    by_pairs(own_in, got_in, pack, t_of, 1, q_out)
    col = lax.broadcasted_iota(jnp.int32, (2 * rows, keys), 1)
    for s in range(seqs):
        valid = col < lengths[s]
        for e in range(tp):
            q = seq_rows(q_out, e, s, seqs, rows)
            keys_in, values_in = keys_values(kv_own, kv_far, e, s, keys)
            mixed = []
            for h in range(2):
                scores = jnp.where(valid, dot(head(q, h), keys_in, NN) * SCALE, MASKED)
                top = jnp.max(scores, axis=1, keepdims=True)
                probs = jnp.exp(scores - top)
                total = jnp.sum(probs, axis=1, keepdims=True)
                mixed.append(dot(probs.astype(BF16), values_in, NT) / total)
                flat = jnp.broadcast_to(top + jnp.log(total), (2 * rows, 128)).T
                row = (s * tp + e) * 2 + h
                lse[row : row + 1, :] = flat[0:1, :]
            both = jnp.where(lanes_of(0), mixed[0], mixed[1]).astype(BF16)
            for j in range(2):
                o_out[e, (j * seqs + s) * rows : (j * seqs + s + 1) * rows, :] = both[
                    j * rows : (j + 1) * rows
                ]
    pairs_back(o_out, pack, t_of, 2, own, send)


def cross_back_kernel(tp, lengths, t_of, own_in, got_in, q_in, lse, kv_own, kv_far, pack, *refs):
    own, send, dq_out, dkv_own, dkv_far, do_s = refs
    seqs, rows = own.shape[0], own.shape[1]
    keys = kv_own.shape[2] // seqs
    by_pairs(own_in, got_in, pack, t_of, 2, do_s)
    key = lax.broadcasted_iota(jnp.int32, (keys, 2 * rows), 0)
    for s in range(seqs):
        valid = key < lengths[s]
        for e in range(tp):
            q, g = seq_rows(q_in, e, s, seqs, rows), seq_rows(do_s, e, s, seqs, rows)
            keys_in, values_in = (v.T for v in keys_values(kv_own, kv_far, e, s, keys))
            dks, dvs, dq = [], [], 0.0
            for h in range(2):
                kh, vh = head(keys_in, h), head(values_in, h)
                row = (s * tp + e) * 2 + h
                scores = dot(kh, q, NT) * SCALE - lse[row : row + 1, :]
                probs = jnp.exp(jnp.where(valid, scores, MASKED))
                dp = dot(vh, g, NT)
                ds = (probs * (dp - jnp.sum(probs * dp, axis=0, keepdims=True))).astype(BF16)
                dvs.append(dot(probs.astype(BF16), g, NN)[:, h * 64 : (h + 1) * 64])
                dks.append(dot(ds, q, NN)[:, h * 64 : (h + 1) * 64] * SCALE)
                dq = dq + dot(ds, kh, TN)
            dq = (dq * SCALE).astype(BF16)
            for j in range(2):
                dq_out[e, (j * seqs + s) * rows : (j * seqs + s + 1) * rows, :] = dq[
                    j * rows : (j + 1) * rows
                ]
            part = slice(s * keys, (s + 1) * keys)
            dkv_own[e, :, part] = jnp.concatenate([dks[0], dvs[0]], axis=1).T.astype(BF16)
            dkv_far[e, :, part] = jnp.concatenate([dks[1], dvs[1]], axis=1).T.astype(BF16)
    pairs_back(dq_out, pack, t_of, 1, own, send)


def ffn_kernel(tp, n_own, n_got, y_own, y_got, weights, *refs):
    active, d_inner, d_own, d_send, o_own, o_send = refs
    seqs, rows = n_own.shape[0], n_own.shape[1]
    half, parts, width = seqs * rows, weights.shape[0], weights.shape[4]
    spans = [slice(i * width, (i + 1) * width) for i in range(parts)]
    n_rows = [chip_rows(n_own, n_got, span) for span in spans]
    y_rows = [chip_rows(y_own, y_got, span) for span in spans]
    for e in range(tp):
        inner = sum(
            dot(n_rows[i], weights[i, e, 0], NT) for i in range(parts)
        )
        grad = sum(
            dot(y_rows[i], weights[i, e, 1], NT) for i in range(parts)
        )
        square = inner * inner
        bend = jnp.tanh(0.7978845608 * (inner + 0.044715 * square * inner))
        active[e] = (0.5 * inner * (1.0 + bend)).astype(BF16)
        slope = 0.5 * (1.0 + bend) + 0.5 * inner * (1.0 - bend * bend) * (
            0.7978845608 * (1.0 + 3.0 * 0.044715 * square)
        )
        d_inner[e] = (grad * slope).astype(BF16)
    for j, (out, send, rows_in) in enumerate(((d_own, d_send, d_inner), (o_own, o_send, active))):
        left = jnp.concatenate([rows_in[e] for e in range(tp)], axis=1)
        for i in range(parts):
            total = dot(left, weights[i, :, j].reshape(left.shape[1], width), NN)
            out[:, :, spans[i]] = total[:half].reshape(seqs, rows, -1)
            send[:, :, spans[i]] = total[half:].astype(BF16).reshape(seqs, rows, -1)


def ffn_grad_kernel(tp, d_near, d_far, a_near, a_far, *refs):
    n_rows, y_rows, out = refs[:4], refs[4:8], refs[8]
    parts, width = out.shape[0], out.shape[4]
    for j, (near, far, given) in enumerate(
        ((d_near, d_far, n_rows), (a_near, a_far, y_rows))
    ):
        right = jnp.concatenate(
            [
                chip_rows(given[0], given[1], slice(None)),
                chip_rows(given[2], given[3], slice(None)),
            ],
            axis=0,
        )
        for e in range(tp):
            left = jnp.concatenate([near[e], far[e]], axis=0)
            value = dot(left, right, TN).astype(BF16)
            for i in range(parts):
                out[i, e, j] = value[:, i * width : (i + 1) * width]


def cross_grad_kernel(tp, dq, o, n_own, n_got, y_own, y_got, dkv_far, keep, send):
    parts, width = keep.shape[1], keep.shape[4]
    for j, (left, a, b) in enumerate(((dq, n_own, n_got), (o, y_own, y_got))):
        right = chip_rows(a, b, slice(None))
        for e in range(tp):
            got = dot(left[e], right, TN)
            for i in range(parts):
                span = slice(i * width, (i + 1) * width)
                keep[e, i, j] = got[0:64, span]
                send[e, (2 * i + j) * 64 : (2 * i + j + 1) * 64] = got[64:128, span].astype(BF16)
    send[:, 2 * parts * 64 :] = dkv_far[...]


def out_grad_kernel(tp, seq_of, own, got, *refs):
    came, (keep, send, acc) = refs[: 2 * tp], refs[2 * tp :]
    rows = own.shape[1]
    acc[...] = jnp.zeros_like(acc)
    for e in range(tp):
        s, mate = seq_of[e], e ^ (tp // 2)
        right = jnp.concatenate([own[s], got[s]], axis=0)
        for ys in range(2):
            left = came[ys * tp + e][...].reshape(2 * rows, -1)
            value = dot(left, right, TN)
            acc[ys, e] += value[0:64]
            acc[ys, mate] += value[64:128]
    keep[...] = acc[0]
    send[...] = acc[1].astype(BF16)


def enc_grad_kernel(n_parts, tp, at, places, d_kv, enc_all, *refs):
    weights, (keep, send, grad_w, all_s) = refs[:n_parts], refs[n_parts:]
    seqs, keys, model = enc_all.shape
    slots = keys // (4 * tp)
    total = 0.0
    for s in range(seqs):
        part = d_kv[:, s * keys : (s + 1) * keys]
        total = total + dot(part, enc_all[s], NN)
        for i in range(n_parts):
            all_s[s, :, span_of(at, i, weights)] = dot(part, weights[i][-d_kv.shape[0] :], TN)
    grad_w[...] = total
    for g in range(4):
        for e in range(tp):
            row = pl.ds(pl.multiple_of(places[g * tp + e] * slots, slots), slots)
            for s in range(seqs):
                if g < 2:
                    keep[g, e, s] = all_s[s, row, :]
                else:
                    send[g - 2, e, s] = all_s[s, row, :].astype(BF16)


def turn_kernel(count, offsets, *refs):
    pieces, outs = refs[:4], refs[4:-1]
    all_s = refs[-1]
    for j, out in enumerate(outs):
        part = pieces[0].shape[1]
        for i in range(4):
            all_s[pl.ds(pl.multiple_of(offsets[i] * part, part), part), :] = pieces[i][j].astype(F32)
        out[...] = all_s[...].T if j < count else all_s[...]


def qkv_grad_kernel(n_parts, tp, at, grads, *refs):
    groups, refs = refs[:4], refs[4:]
    weights, outs, sums = refs[:n_parts], refs[n_parts:-1], refs[-1]
    rows, columns = grads.shape[1], grads.shape[2]
    left = [grads[g * tp : (g + 1) * tp].reshape(-1, columns) for g in range(4)]
    ones = jnp.ones((8, left[0].shape[0]), BF16)
    counts = sum(dot(ones, part, NN) for part in left)
    turned = [part.T for part in left]
    for i in range(n_parts):
        span = span_of(at, i, outs)
        total = 0.0
        for g in range(4):
            right = groups[g][:, :rows, span].reshape(left[g].shape[0], -1)
            total = total + dot(turned[g], right, NN)
        outs[i][...] = total.astype(outs[i].dtype)
        weight = weights[i][0:columns].astype(F32)
        sums[0:1, span] = jnp.sum(total * weight, axis=0, keepdims=True)
        sums[1:2, span] = dot(counts, weight, NN, lax.Precision.HIGHEST)[0:1]


def self_back_kernel(n_parts, tp, block, at, order, qkv, lse, *refs):
    outs, grads, refs = refs[: 2 * tp], refs[2 * tp : 4 * tp], refs[4 * tp :]
    weights, (grad_qkv, keep, send, g_s, sum_s, dq_s) = refs[:n_parts], refs[n_parts:]
    length, width = qkv.shape[1], qkv.shape[2]
    rows = outs[0].shape[1]
    lane8 = lax.broadcasted_iota(jnp.int32, (8, width), 1)
    row8 = lax.broadcasted_iota(jnp.int32, (8, width), 0)
    chosen = jnp.where(lane8 // (width // 2) == row8, 1.0, 0.0).astype(F32)
    for j in range(2 * tp):
        for kr in range(2):
            r = kr * 2 * tp + j
            here = pl.ds(pl.multiple_of(order[r] * rows, rows), rows)
            g_s[here, :] = grads[j][kr]
            sum_s[:, here] = dot(
                chosen,
                grads[j][kr].astype(F32) * outs[j][kr].astype(F32),
                NT,
                lax.Precision.HIGHEST,
            )
    row = lax.broadcasted_iota(jnp.int32, (block, block), 0)
    col = lax.broadcasted_iota(jnp.int32, (block, block), 1)
    dq_s[...] = jnp.zeros_like(dq_s)
    blocks = length // block
    for j in range(blocks):
        here = slice(j * block, (j + 1) * block)
        kj, vj = qkv[1, here, :], qkv[2, here, :]
        dks, dvs = [], []
        for h in range(2):
            kh, vh = head(kj, h), head(vj, h)
            dk = dv = 0.0
            for i in range(j, blocks):
                there = slice(i * block, (i + 1) * block)
                q, g = qkv[0, there, :], g_s[there, :]
                scores = dot(kh, q, NT) * SCALE - lse[h : h + 1, there]
                if i == j:
                    scores = jnp.where(col >= row, scores, MASKED)
                probs = jnp.exp(scores)
                ds = (probs * (dot(vh, g, NT) - sum_s[h : h + 1, there])).astype(BF16)
                dv, dk = dv + dot(probs.astype(BF16), g, NN), dk + dot(ds, q, NN)
                dq_s[there, :] += dot(ds, kh, TN)
            dks.append(dk)
            dvs.append(dv)
        dk = (jnp.where(lanes_of(0), dks[0], dks[1]) * SCALE).astype(BF16)
        dv = jnp.where(lanes_of(0), dvs[0], dvs[1]).astype(BF16)
        qkv_rows = block // rows
        for t in range(qkv_rows):
            r, part = order[4 * tp + j * qkv_rows + t], slice(t * rows, (t + 1) * rows)
            grad_qkv[r, :, width : 2 * width] = dk[part]
            grad_qkv[r, :, 2 * width : 3 * width] = dv[part]
    for p in range(4 * tp):
        grad_qkv[order[4 * tp + p], :, 0:width] = (
            dq_s[p * rows : (p + 1) * rows, :] * SCALE
        ).astype(BF16)
    for g in (2, 3, 0, 1):
        left = grad_qkv[g * tp : (g + 1) * tp].reshape(tp * rows, -1)
        for i in range(n_parts):
            span = span_of(at, i, weights)
            value = dot(left, weights[i][0 : 3 * width], NN).reshape(tp, rows, -1)
            if g < 2:
                keep[g, :, :, span] = value.astype(BF16)
            else:
                send[g - 2, :, :, span] = value.astype(BF16)


def swap(value, axis, bit):
    return lax.ppermute(value, axis, [(i, i ^ bit) for i in range(lax.axis_size(axis))])


def swap_core(value):
    return swap(value, "ctx", 1)


def swap_y(value):
    return swap(value, "ctx", 2)


def from_tp(value, step):
    return swap(value, "tp", step)


def from_chip(value, far, step):
    ctx, size = lax.axis_size("ctx"), lax.axis_size("tp")
    if far == 0 and step == 0:
        return value
    pairs = [
        ((c ^ (2 * far)) * size + (i ^ step), c * size + i)
        for c in range(ctx)
        for i in range(size)
    ]
    return lax.ppermute(value, ("ctx", "tp"), pairs)


def after(value, *others):
    return lax.optimization_barrier((value, others))[0]


def pick(value, index, axis):
    return lax.dynamic_index_in_dim(value, index, axis, keepdims=False)


def gather_tp(value):
    return jnp.stack([value] + [from_tp(value, e) for e in range(1, lax.axis_size("tp"))])


def model_parts(value):
    if lax.axis_size("fsdp") == 2:
        return (value, swap(value, "fsdp", 1))
    return (lax.all_gather(value, "fsdp", axis=value.ndim - 1, tiled=True),)


def sum_model(value):
    if lax.axis_size("fsdp") != 2:
        return lax.psum_scatter(
            value.astype(BF16), "fsdp", scatter_dimension=value.ndim - 1, tiled=True
        ).astype(F32)
    width, mine = value.shape[-1] // 2, lax.axis_index("fsdp")
    keep = lax.dynamic_slice_in_dim(value, mine * width, width, value.ndim - 1)
    send = lax.dynamic_slice_in_dim(value, (1 - mine) * width, width, value.ndim - 1)
    return keep.astype(F32) + swap(send.astype(BF16), "fsdp", 1).astype(F32)


def sum_parts(parts):
    if len(parts) == 1:
        return sum_model(parts[0])
    return parts[0].astype(F32) + swap(parts[1], "fsdp", 1).astype(F32)


def sum_tp(pieces):
    total = pieces[0].astype(F32)
    for e in range(1, lax.axis_size("tp")):
        total = total + from_tp(pieces[e].astype(BF16), e).astype(F32)
    return total


def sum_all(value):
    for axis in ("ctx", "tp", "fsdp"):
        if axis == "fsdp" and lax.axis_size(axis) != 2:
            value = lax.psum(value, axis)
            continue
        bit = 1
        while bit < lax.axis_size(axis):
            value = value + swap(value, axis, bit)
            bit *= 2
    return value


def shards(
    tokens,
    enc_states,
    enc_lengths,
    cotangent,
    gain_self,
    shift_self,
    w_query,
    w_key,
    w_value,
    w_out,
    gain_cross,
    shift_cross,
    cross_query,
    cross_key,
    cross_value,
    cross_out,
    gain_ffn,
    shift_ffn,
    w_inner,
    w_outer,
):
    seqs, rows, model = tokens.shape
    tp, ctx = lax.axis_size("tp"), lax.axis_size("ctx")
    z, c = lax.axis_index("tp"), lax.axis_index("ctx")
    y, k = c // 2, c % 2
    span = tp // 2
    local = w_query.shape[0]
    hid = w_inner.shape[1] // ctx
    own_rows = tokens.shape
    chip = 2 * seqs * rows
    n_parts = 2 if lax.axis_size("fsdp") == 2 else 1
    mine = lax.axis_index("fsdp") * local if n_parts == 2 else 0
    at = jnp.stack([jnp.int32(mine), jnp.int32(model // 2 - mine)])
    step = jnp.arange(tp, dtype=jnp.int32)
    seq_of = (z ^ step) // span
    two = lambda vector: vector.reshape(1, -1)
    gains = [two(g) for g in (gain_self, shift_self, gain_cross, shift_cross, gain_ffn, shift_ffn)]

    rel = jnp.arange(4 * tp, dtype=jnp.int32)
    places = (2 * ((rel // tp) % 2 ^ y) + ((rel // (2 * tp)) ^ k)) * tp + ((rel % tp) ^ z)
    order = ((((rel // tp) % 2) ^ k) * 2 + ((rel // (2 * tp)) ^ y)) * tp + ((rel % tp) ^ z)
    places, order = places.astype(jnp.int32), order.astype(jnp.int32)

    def own_head(weight):
        return lax.dynamic_slice_in_dim(weight, c * HEAD_DIM, HEAD_DIM, 0)

    def core_half(weight):
        other = lax.dynamic_slice_in_dim(weight, (c ^ 2) * HEAD_DIM, HEAD_DIM, 0)
        return jnp.concatenate([own_head(weight), other])

    own_qkv = jnp.stack([own_head(w.T) for w in (w_query, w_key, w_value)])
    own_ckv = jnp.concatenate([own_head(cross_key.T), own_head(cross_value.T)])
    own_qkv, picks = lax.optimization_barrier((own_qkv, (z ^ step) // span))
    other_qkv = from_tp(own_qkv, span)
    slots = enc_states.shape[1]
    keys = 4 * tp * slots
    pieces = kernel_call(
        functools.partial(first_norm_kernel, tp),
        "norm_self",
        [picks],
        [tokens, enc_states, gains[0], gains[1]],
        [shape((rows + seqs * slots, model), BF16)] * tp,
        [pltpu.VMEM(own_rows, BF16)],
    )
    t_of = (z ^ step).astype(jnp.int32)
    pack = jnp.concatenate([core_half(w) for w in (w_out, cross_query.T, cross_out)])

    def gather_weights(value):
        got = lax.all_gather(value, ("fsdp", "tp"))
        got = got.reshape(-1, tp, *value.shape)
        if n_parts == 2:
            return got
        return jnp.moveaxis(got, 0, -2).reshape(1, tp, *value.shape[:-1], model)

    which = jnp.stack([c, c ^ 1, c ^ 2, c ^ 3]).astype(jnp.int32)
    near = [pieces[0]] + [None] * (tp - 1)
    bit = span
    while bit:
        for e in range(0, tp, 2 * bit):
            near[e + bit] = from_tp(pieces[bit] if e == 0 else near[e], bit)
        bit //= 2
    far = [swap_y(piece) for piece in near]
    near = jnp.stack(after(near, other_qkv, far[0]))
    h_qkv = model_parts(
        jnp.concatenate([jnp.stack([own_qkv, other_qkv], 1).reshape(-1, local), own_ckv])
    )
    far = after(jnp.stack(far), h_qkv)
    groups = [near, far, swap_core(near), swap_core(far)]

    h_ffn = jnp.stack(
        [
            lax.dynamic_slice_in_dim(w_inner, c * hid, hid, 1).T,
            lax.dynamic_slice_in_dim(w_outer, c * hid, hid, 0),
        ]
    )
    pack = gather_weights(after(pack, near))
    h_ffn = gather_weights(after(h_ffn, near))
    y_far = swap_y(after(cotangent, far))
    y_rows = [cotangent, swap_core(after(cotangent, near)), y_far]

    enc_all, kv_own = kernel_call(
        functools.partial(keys_kernel, n_parts, tp),
        "cross_keys",
        [at, places],
        [*groups, *h_qkv],
        [shape((seqs, keys, model), BF16), shape((2 * HEAD_DIM, seqs * keys), BF16)],
        flops=4 * seqs * keys * model * 2 * HEAD_DIM,
    )
    kv_at = kv_own
    kv_own = gather_tp(kv_own)

    length, width = ctx * tp * rows, 2 * HEAD_DIM
    qkv, lse_self, *o_sent = kernel_call(
        functools.partial(self_kernel, n_parts, tp, BLOCK),
        "self_attend",
        [after(at, kv_at), places, order],
        [*groups, *h_qkv],
        [shape((3, length, width), BF16), shape((2, length), F32)]
        + [shape((2, rows, width), BF16)] * (2 * tp),
        [pltpu.VMEM((4 * tp, rows, width), BF16)],
        flops=4 * length * length * width + 6 * length * model * width,
    )
    o_sent = after(o_sent, kv_own, y_far)
    kv_far = swap_y(kv_own)
    came = [
        from_chip(o_sent[ys * tp + e], ys, e) for ys in range(2) for e in range(tp)
    ]
    partial_own, partial_send = kernel_call(
        functools.partial(out_kernel, tp),
        "out_self",
        [t_of, seq_of],
        [*came, pack],
        [shape(own_rows, F32), shape(own_rows, BF16)],
        [pltpu.VMEM(own_rows, F32)],
        flops=2 * chip * 4 * width * model,
    )

    def add_norm(before, own, sent, which):
        return kernel_call(
            norm_kernel,
            "add_norm",
            [],
            [before, own, swap_core(sent), gains[2 * which], gains[2 * which + 1]],
            [shape(own_rows, F32), shape(own_rows, BF16)],
        )

    hidden1, n2 = add_norm(tokens, partial_own, partial_send, 1)

    n2_got = swap_core(n2)
    partial_own, partial_send, q_cross, o_cross, lse_cross = kernel_call(
        functools.partial(cross_kernel, tp),
        "cross_attend",
        [enc_lengths, t_of],
        [n2, n2_got, kv_own, kv_far, pack],
        [
            shape(own_rows, F32),
            shape(own_rows, BF16),
            shape((tp, chip, width), BF16),
            shape((tp, chip, width), BF16),
            shape((seqs * tp * 2, 2 * rows), F32),
        ],
        flops=4 * chip * tp * width * (model + keys),
    )
    hidden2, n3 = add_norm(hidden1, partial_own, partial_send, 2)

    n3_far = swap_y(n3)
    y_rows.append(swap_core(after(y_far, n3)))
    n_rows = [n3, swap_core(n3), n3_far, swap_core(n3_far)]

    def feed(first):
        return kernel_call(
            functools.partial(ffn_kernel, tp),
            "feed_forward",
            [],
            [*n_rows[first : first + 2], *y_rows[first : first + 2], h_ffn],
            [shape((tp, chip, hid), BF16)] * 2 + [shape(own_rows, F32), shape(own_rows, BF16)] * 2,
            flops=8 * chip * model * tp * hid,
        )

    a_far, d_far, dn_far, dn_far_send, out_far, out_far_send = feed(2)
    a_near, d_near, dn_own, dn_near_send, out_own, out_near_send = feed(0)

    def far_sum(own, sent):
        return (own + swap_core(sent).astype(F32)).astype(BF16)

    dn_near = swap_core(dn_near_send)
    dn_far = far_sum(dn_far, dn_far_send)
    g_ffn = kernel_call(
        functools.partial(ffn_grad_kernel, tp),
        "grad_feed_forward",
        [],
        [after(d_near, dn_far, dn_near), d_far, a_near, a_far, *n_rows, *y_rows],
        [shape((n_parts, tp, 2, hid, model // n_parts), BF16)],
        flops=8 * chip * model * tp * hid,
    )[0]
    dn_far = swap_y(dn_far)

    def norm_back(hidden, gain, before, own, *got):
        return kernel_call(
            norm_back_kernel,
            "norm_back",
            [],
            [hidden, gain, before, own, *got],
            [shape(own_rows, F32), shape(own_rows, BF16), shape((2, model), F32)],
        )

    grad2, y2, sums_ffn = norm_back(
        hidden2, after(gains[4], g_ffn), cotangent, dn_own, dn_near, dn_far
    )
    if n_parts == 1:
        g_ffn = g_ffn.reshape(tp, 2, hid, -1, local).transpose(3, 0, 1, 2, 4)
    g_ffn = lax.psum_scatter(
        after(g_ffn.reshape(-1, 2, hid, local), dn_far), ("fsdp", "tp"), scatter_dimension=0
    )
    g_ffn = lax.all_gather(g_ffn.astype(BF16), "ctx", axis=1, tiled=True)

    y2_got = swap_core(y2)
    held, out_near_send, out_far_send = after((out_far, out_near_send, out_far_send), y2)
    out_near, out_far = swap_core(out_near_send), far_sum(held, out_far_send)
    dn_own, dn_send, dq_cross, dkv_own, dkv_far = kernel_call(
        functools.partial(cross_back_kernel, tp),
        "cross_attend_back",
        [enc_lengths, after(t_of, out_near, out_far)],
        [y2, y2_got, q_cross, lse_cross, kv_own, kv_far, pack],
        [
            shape(own_rows, F32),
            shape(own_rows, BF16),
            shape((tp, chip, width), BF16),
            shape(kv_own.shape, BF16),
            shape(kv_own.shape, BF16),
        ],
        [pltpu.VMEM((tp, chip, width), BF16)],
        flops=4 * chip * tp * width * (model + 3 * keys),
    )
    out_far = swap_y(out_far)
    dn_send = after(dn_send, out_far)
    dn_got = swap_core(dn_send)
    half = seqs * keys
    halves = model // half
    keep, send = kernel_call(
        functools.partial(cross_grad_kernel, tp),
        "grad_cross",
        [],
        [dq_cross, o_cross, n2, n2_got, y2, y2_got, dkv_far],
        [
            shape((tp, halves, 2, HEAD_DIM, half), F32),
            shape((tp, 2 * halves * HEAD_DIM + width, half), BF16),
        ],
        flops=4 * chip * tp * width * model,
    )
    cross_got = swap_y(send)
    grad1, y1, sums_cross = norm_back(hidden1, gains[2], grad2, dn_own, dn_got)

    y1_got = swap_core(y1)
    do_sent = kernel_call(
        functools.partial(grad_mixed_kernel, tp),
        "grad_mixed",
        [t_of, seq_of],
        [y1, y1_got, pack],
        [shape((2, rows, width), BF16)] * (2 * tp),
        flops=2 * chip * 4 * width * model,
    )
    do_came = [
        from_chip(do_sent[ys * tp + e], ys, e) for ys in range(2) for e in range(tp)
    ]
    out_keep, out_send = kernel_call(
        functools.partial(out_grad_kernel, tp),
        "grad_out",
        [after(seq_of, do_sent)],
        [y1, y1_got, *came],
        [shape((tp, HEAD_DIM, model), F32), shape((tp, HEAD_DIM, model), BF16)],
        [pltpu.VMEM((2, tp, HEAD_DIM, model), F32)],
        flops=2 * chip * tp * width * model,
    )
    cross_got = after(cross_got, do_came)
    g_cross = keep + cross_got[:, :-width].reshape(keep.shape).astype(F32)
    d_kv = dkv_own.astype(F32) + cross_got[:, -width:].astype(F32)
    first = lax.axis_index("fsdp") if n_parts == 2 else 0
    cross_x = swap(pick(g_cross, 1 - first, 1).astype(BF16), "fsdp", 1) if n_parts == 2 else None
    out_got = swap_y(after(out_send, do_came))
    d_qkv, dn_keep, dn_send = kernel_call(
        functools.partial(self_back_kernel, n_parts, tp, BLOCK),
        "self_attend_back",
        [after(at, out_keep, g_cross), jnp.concatenate([places, order])],
        [qkv, lse_self, *o_sent, *do_came, *h_qkv],
        [
            shape((4 * tp, rows, 3 * width), BF16),
            shape((2, tp, rows, model), BF16),
            shape((2, tp, rows, model), BF16),
        ],
        [
            pltpu.VMEM((length, width), BF16),
            pltpu.VMEM((8, length), F32),
            pltpu.VMEM((length, width), F32),
        ],
        flops=10 * length * length * width + 6 * length * model * width,
    )
    dn_send, dn_keep, cross_x, out_got, out_far = after(
        (dn_send, dn_keep, cross_x, out_got, out_far), d_qkv
    )
    dn_got = swap_core(dn_send)
    dn_sent = [(dn_keep[1, e].astype(F32) + dn_got[1, e].astype(F32)).astype(BF16) for e in range(tp)]
    dn_near = [
        dn_keep[0, e].astype(F32) + dn_got[0, e].astype(F32) for e in range(tp)
    ]
    g_cross, d_kv, cross_x, out_got, out_far = after(
        (g_cross, d_kv, cross_x, out_got, out_far), dn_sent
    )
    dn_upper = swap_y(jnp.stack(dn_sent[span:]))
    dn_lower = swap_y(jnp.stack(dn_sent[:span]))
    if n_parts == 2:
        g_cross = pick(g_cross, first, 1) + cross_x.astype(F32)
        g_cross = sum_tp(jnp.concatenate([g_cross.reshape(tp, -1, local), d_kv], axis=1))
        g_cross = after(g_cross, dn_upper)
        g_cross, d_kv = g_cross[: 2 * HEAD_DIM].reshape(2, HEAD_DIM, local), g_cross[2 * HEAD_DIM :]
    else:
        g_cross = sum_tp(
            sum_model(g_cross.transpose(0, 2, 3, 1, 4).reshape(tp, 2, HEAD_DIM, model))
        )
        d_kv = sum_tp(d_kv)
    out_tokens = (hidden2 + out_own + out_near.astype(F32) + out_far.astype(F32)).astype(BF16)
    grad_inner, grad_outer = after(g_ffn[0], dn_sent).T.astype(F32), g_ffn[1].astype(F32)
    *g_qkv, sums_self = kernel_call(
        functools.partial(qkv_grad_kernel, n_parts, tp),
        "grad_qkv",
        [after(at, dn_upper, grad_inner, grad_outer)],
        [d_qkv, *groups, *h_qkv],
        (
            [shape((3 * width, model), F32)]
            if n_parts == 1
            else [shape((3 * width, local), F32), shape((3 * width, local), BF16)]
        )
        + [shape((2, model), F32)],
        flops=6 * length * width * model,
    )
    enc_keep, enc_send, g_ckv = kernel_call(
        functools.partial(enc_grad_kernel, n_parts, tp),
        "grad_enc",
        [at, places],
        [d_kv.astype(BF16), enc_all, *h_qkv],
        [
            shape((2, tp, seqs, slots, model), F32),
            shape((2, tp, seqs, slots, model), BF16),
            shape((2 * HEAD_DIM, model), F32),
        ],
        [pltpu.VMEM((seqs, keys, model), F32)],
        flops=4 * seqs * keys * width * model,
    )
    enc_got = swap_core(enc_send)
    enc_far = swap_y((enc_keep[1] + enc_got[1].astype(F32)).astype(BF16))
    grad_enc = sum_tp(enc_keep[0] + enc_got[0].astype(F32) + enc_far.astype(F32))
    g_out = sum_model(out_keep + out_got.astype(F32))
    dn_pieces = [dn_near[e] + dn_lower[e].astype(F32) for e in range(span)]
    dn_pieces += [dn_near[span + e] + dn_upper[e].astype(F32) for e in range(span)]
    for first_piece in (span, 0):
        count = span
        while count > 1:
            count //= 2
            for e in range(count):
                got = from_tp(dn_pieces[first_piece + count + e].astype(BF16), count)
                if first_piece:
                    dn_began = got
                dn_pieces[first_piece + e] = dn_pieces[first_piece + e] + got.astype(F32)
    dn_other = from_tp(dn_pieces[span].astype(BF16), span)
    grad_tokens = kernel_call(
        last_norm_kernel,
        "norm_back_self",
        [seq_of],
        [tokens, gains[0], grad1, dn_pieces[0], dn_other],
        [shape(own_rows, F32)],
        [pltpu.VMEM(own_rows, F32)],
    )[0]

    sums = jnp.concatenate([sums_self, sums_cross, sums_ffn])
    sums = sum_all(after(sums, dn_other))
    grad_shift_self = sums[1]
    grad_gain_self = (sums[0] - shift_self * sums[1]) / gain_self

    def turned(pieces, count):
        quarters = pieces[0].shape[0]
        return kernel_call(
            functools.partial(turn_kernel, count),
            "turn",
            [which],
            pieces,
            [
                shape((pieces[0].shape[2], 4 * pieces[0].shape[1])[:: 1 if j < count else -1], F32)
                for j in range(quarters)
            ],
            [pltpu.VMEM((4 * pieces[0].shape[1], pieces[0].shape[2]), F32)],
        )

    def along_ctx(value):
        far = swap_y(value)
        return [value, swap_core(value), far, swap_core(far)]


    g_cross = jnp.concatenate([sum_model(g_ckv).reshape(2, HEAD_DIM, local), g_cross]).astype(BF16)
    g_cross = lax.all_gather(g_cross, "ctx", axis=1, tiled=True).astype(F32)
    g_qkv, g_out = after((sum_parts(g_qkv), g_out), dn_began)
    g_qkv = g_qkv.reshape(3, 2, HEAD_DIM, local)
    total, g_mate = g_out[0], g_qkv[:, 1].reshape(-1, local)
    for e in range(1, tp):
        piece = g_out[e]
        if e == span:
            got = from_tp(jnp.concatenate([piece, g_mate]).astype(BF16), e).astype(F32)
            total, g_mate = total + got[:HEAD_DIM], got[HEAD_DIM:]
        else:
            total = total + from_tp(piece.astype(BF16), e).astype(F32)
    g_qkv = g_qkv[:, 0] + g_mate.reshape(3, HEAD_DIM, local)
    g_self = jnp.concatenate([g_qkv, total[None]]).astype(BF16)
    g_self = turned(along_ctx(g_self), 3)
    return (
        out_tokens,
        grad_tokens,
        grad_enc,
        grad_gain_self,
        grad_shift_self,
        g_self[0],
        g_self[1],
        g_self[2],
        g_self[3],
        sums[2],
        sums[3],
        g_cross[2].T,
        g_cross[0].T,
        g_cross[1].T,
        g_cross[3],
        sums[4],
        sums[5],
        grad_inner,
        grad_outer,
    )


def solution(mesh):
    in_specs = (
        P("fsdp", ("ctx", "tp"), None),
        P("fsdp", ("ctx", "tp"), None),
        P("fsdp"),
        P("fsdp", ("ctx", "tp"), None),
        P(),
        P(),
        P("fsdp", "tp"),
        P("fsdp", "tp"),
        P("fsdp", "tp"),
        P("tp", "fsdp"),
        P(),
        P(),
        P("fsdp", "tp"),
        P("fsdp", "tp"),
        P("fsdp", "tp"),
        P("tp", "fsdp"),
        P(),
        P(),
        P("fsdp", "tp"),
        P("tp", "fsdp"),
    )
    out_specs = (
        P("fsdp", ("ctx", "tp"), None),
        P("fsdp", ("ctx", "tp"), None),
        P("fsdp", ("ctx", "tp"), None),
        P(),
        P(),
        P("fsdp", "tp"),
        P("fsdp", "tp"),
        P("fsdp", "tp"),
        P("tp", "fsdp"),
        P(),
        P(),
        P("fsdp", "tp"),
        P("fsdp", "tp"),
        P("fsdp", "tp"),
        P("tp", "fsdp"),
        P(),
        P(),
        P("fsdp", "tp"),
        P("tp", "fsdp"),
    )
    return jax.shard_map(shards, mesh=mesh, in_specs=in_specs, out_specs=out_specs, check_vma=False)
```
